32 devices in a mesh: group: 2 (over y), tm: 4 (over z), tensor: 2 (over x), pair: 2 (over core).
Axes of the slice: x: 2, y: 2, z: 4, core: 2. Of those that a mesh axis runs over, the one named last changes fastest.
Arguments:
- frames: bfloat16 [12288, 1536], P(('group', 'tm'), ('tensor', 'pair')), parts along dimension 0, may hold values from -6 to 6
- router_weight: float32 [1536], replicated, may hold values from -0.15625 to 0.15625
- norm_gain: float32 [1536], replicated, may hold values from 0.25 to 1.75
- up_weight: bfloat16 [1536, 3072], P(None, ('tensor', 'pair')), may hold values from -0.15625 to 0.15625
- down_weight: bfloat16 [3072, 1536], P(('tensor', 'pair')), may hold values from -0.15625 to 0.15625
- picked_rows: int32 [3072], P(('group', 'tm')), parts along dimension 0, may hold values from 0 to 1535, as said below
- picked_count: int32 [8], P('group'), parts along dimension 0, may hold values from 1 to 384, 768 in all
- cotangent: bfloat16 [12288, 1536], P(('group', 'tm'), ('tensor', 'pair')), parts along dimension 0, may hold values from -6 to 6
Outputs:
- mixed: bfloat16 [12288, 1536], P(('group', 'tm'), ('tensor', 'pair')), parts along dimension 0
- frames_grad: bfloat16 [12288, 1536], P(('group', 'tm'), ('tensor', 'pair')), parts along dimension 0
The draws below stay inside these ranges and needn't reach their ends.
There are 2 independent parts, one for each index of `group`. The reference program is written for one: setup_inputs(seed, part) draws one part's arguments, and reference() takes and returns one part's arrays. A program takes and returns all parts, laid end to end along the dimension named above; an argument that names none is the same for every part. Nothing has to cross between parts.
Inputs may be any that keep to these rules, and one draw needn't show every extreme that they name: `picked_rows`: the 384 entries of one index of tm are distinct frame indices among its own 1536 frames; the first picked_count of them are its routed frames, the others are not used. `picked_count`: the counts sum to 768.
All inputs are finite; a program needn't handle non-finite values.
Results may differ from the reference program's by a relative error of at most 0.0028.
Values may be sent and summed in bfloat16 or wider, within the bound.
No kernel may reach another device: no remote copies, remote signals or barrier semaphores. Data moves between devices by JAX's collectives and lax.ppermute only.
A program may use at most 64 MiB of HBM per device.

```python
import math
import jax
import jax.numpy as jnp
import numpy as np
from jax import lax

D = 1536
FF = 3072
FR_DEV = 1536
SEL = 192
CAP = 384
FRAMES = 6144
N_TM = 4


def draw_picked_rows(key, part):
    key = jax.random.fold_in(key, 7)
    noise = jax.random.randint(key, (N_TM, FR_DEV), 0, 1 << 18)
    scores = noise * FR_DEV + jnp.arange(FR_DEV, dtype=jnp.int32)[None, :]
    order = jnp.argsort(scores, axis=1)
    return order[:, :CAP].reshape(N_TM * CAP).astype(jnp.int32)


def strengthened(array, stream_key, source, target, parts, factor):
    def block_of(axis_at):
        return (jnp.arange(array.shape[axis_at]) // (array.shape[axis_at] // parts)).reshape((-1,) + (1,) * (array.ndim - 1 - axis_at))

    near = jax.random.permutation(stream_key, parts)[block_of(target)]
    other_side = (block_of(target) + parts // 2) % parts
    return jnp.where((block_of(source) == near) | (block_of(source) == other_side), factor * array, array)


def levels(own_key, extent, split, least, largest):
    def one(dim, parts):
        draws = jax.random.uniform(jax.random.fold_in(jax.random.fold_in(own_key, 6), dim), (parts,), jnp.float32, least / len(split), largest / len(split))
        return jnp.repeat(jnp.exp(draws), extent[dim] // parts).reshape((-1,) + (1,) * (len(extent) - dim - 1))

    loudness = one(*split[0])
    for cut in split[1:]:
        loudness = loudness * one(*cut)
    return loudness


def length_profile(amount, total, most, lean):
    loads = [(1 << 20) // math.isqrt(standing ** lean) + 1 for standing in range(2, amount + 1)]
    surplus, holding = total - most - (amount - 1), [1] * (amount - 1)
    while surplus > 0:
        candidates = [i for i in range(amount - 1) if holding[i] < most]
        pool, budget = sum([loads[i] for i in candidates]), surplus
        for i in candidates:
            more = min(most - holding[i], max(1, budget * loads[i] // pool), surplus)
            holding[i] = holding[i] + more
            surplus = surplus - more
    return np.array([most] + holding)


def uneven_parts(own_key, number_of, total, bound, lean):
    if number_of == 2:
        one = jax.random.randint(own_key, (), max(1, total - bound), min(bound, total - 1) + 1)
        return jnp.stack([one, total - one])
    tallies = jnp.asarray(length_profile(number_of, total, bound, lean), jnp.int32)
    couples = (number_of - 1) // 2
    source_of, taker = tallies[1:1 + 2 * couples:2], tallies[2:2 + 2 * couples:2]
    slack = jnp.minimum(source_of - 1, bound - taker)
    moved = jax.random.randint(jax.random.fold_in(own_key, 1), (couples,), 0, 1 << 20) % (slack + 1)
    tallies = tallies.at[1:1 + 2 * couples:2].set(source_of - moved).at[2:2 + 2 * couples:2].set(taker + moved)
    return tallies[jax.random.permutation(jax.random.fold_in(own_key, 2), number_of)]


def gaussian(key, dims, width, limit, shards=(), kind=jnp.bfloat16):
    factor_of = levels(key, dims, shards, -0.22, 0.18) if shards else 1.0
    result = jax.random.normal(key, dims, jnp.float32) * width * factor_of
    return jnp.minimum(jnp.maximum(result, -limit), limit).astype(kind)


def heavy_noise(own_key, extent, spread, limit, pieces, heavy, held_as=jnp.bfloat16):
    entries = spread * jax.random.normal(own_key, extent, jnp.float32)
    if pieces:
        entries = entries * levels(own_key, extent, pieces, -0.22, 0.18)
    return jnp.clip(strengthened(entries, jax.random.fold_in(own_key, 3), *heavy), -limit, limit).astype(held_as)


def setup_inputs(seed: int = 0, part: int = 0) -> dict:
    seeds = jax.random.split(jax.random.key(seed), 9)
    part_keys = jax.random.split(jax.random.fold_in(seeds[8], part), 9)
    frames = gaussian(part_keys[0], (FRAMES, D), 1.0, 6.0, ((0, 4), (1, 4)))
    router_weight = gaussian(seeds[1], (D,), D ** -0.5, 0.15625, (), jnp.float32)
    norm_gain = jnp.clip(1.0 + 0.15 * jax.random.normal(seeds[2], (D,), jnp.float32), 0.25, 1.75)
    up_weight = gaussian(seeds[3], (D, FF), D ** -0.5, 0.15625, ((1, 4),))
    down_weight = heavy_noise(seeds[4], (FF, D), FF ** -0.5, 0.15625, ((0, 4),), (0, 1, 4, 2.0))
    picked_rows = draw_picked_rows(jax.random.fold_in(jax.random.fold_in(seeds[8], part), 71), part)
    picked_count = uneven_parts(part_keys[6], N_TM, N_TM * SEL, CAP, 2).astype(jnp.int32)
    cotangent = gaussian(part_keys[7], (FRAMES, D), 1.0, 6.0, ((0, 4), (1, 4)))
    return {"frames": frames, "router_weight": router_weight, "norm_gain": norm_gain, "up_weight": up_weight, "down_weight": down_weight, "picked_rows": picked_rows, "picked_count": picked_count, "cotangent": cotangent}


def reference(frames, router_weight, norm_gain, up_weight, down_weight, picked_rows, picked_count, cotangent):
    all_ranks = N_TM * SEL
    highest = lax.Precision.HIGHEST
    rank_ends = jnp.cumsum(picked_count).astype(jnp.int32)
    rank_starts = (rank_ends - picked_count).astype(jnp.int32)
    my_ranks = jnp.arange(all_ranks, dtype=jnp.int32)
    owners = lax.optimization_barrier(jnp.sum((rank_ends[None, :] <= my_ranks[:, None]).astype(jnp.int32), axis=1))
    slot_of = my_ranks - rank_starts[owners]
    local_row = picked_rows.reshape(N_TM, CAP)[owners, slot_of]
    row_index = (owners * FR_DEV + local_row).astype(jnp.int32)
    rows_in = frames[row_index].astype(jnp.float32)
    rows_cot = cotangent[row_index].astype(jnp.float32)
    gate_score = jax.nn.sigmoid(lax.optimization_barrier(jnp.sum(rows_in * router_weight, axis=-1)))
    row_mean = lax.optimization_barrier(jnp.mean(rows_in, axis=-1, keepdims=True))
    deviate = rows_in - row_mean
    inv_std = lax.rsqrt(lax.optimization_barrier(jnp.mean(deviate * deviate, axis=-1, keepdims=True)) + 1e-05)
    centred = deviate * inv_std
    normed = (centred * norm_gain).astype(jnp.bfloat16)
    up_full = up_weight.astype(jnp.float32)
    down_full = down_weight.astype(jnp.float32)
    hidden_in = jnp.dot(normed.astype(jnp.float32), up_full, precision=highest)
    hidden = jax.nn.silu(hidden_in).astype(jnp.bfloat16)
    ffn_out = jnp.dot(hidden.astype(jnp.float32), down_full, precision=highest)
    routed_out = (0.5 * gate_score[:, None] * ffn_out).astype(jnp.bfloat16)
    mixed = frames.astype(jnp.float32).at[row_index].add(routed_out.astype(jnp.float32)).astype(jnp.bfloat16)
    grad_hid = jnp.dot(rows_cot, down_full.T, precision=highest)
    grad_score = 0.5 * lax.optimization_barrier(jnp.sum(grad_hid * hidden.astype(jnp.float32), axis=-1))
    swish_gate = jax.nn.sigmoid(hidden_in)
    grad_pre = (0.5 * gate_score[:, None] * grad_hid * swish_gate * (1.0 + hidden_in * (1.0 - swish_gate))).astype(jnp.bfloat16)
    grad_normed = jnp.dot(grad_pre.astype(jnp.float32), up_full.T, precision=highest)
    grad_scaled = grad_normed * norm_gain
    plain_mean = lax.optimization_barrier(jnp.mean(grad_scaled, axis=-1, keepdims=True))
    cross_mean = lax.optimization_barrier(jnp.mean(grad_scaled * centred, axis=-1, keepdims=True))
    router_term = (grad_score * gate_score * (1.0 - gate_score))[:, None] * router_weight
    grad_rows = (inv_std * (grad_scaled - plain_mean - centred * cross_mean) + router_term).astype(jnp.bfloat16)
    frames_grad = cotangent.astype(jnp.float32).at[row_index].add(grad_rows.astype(jnp.float32)).astype(jnp.bfloat16)
    return (mixed, frames_grad)
```

```python
import functools

import jax
import jax.numpy as jnp
from jax import lax
from jax.experimental import pallas as pl
from jax.experimental.pallas import tpu as pltpu
from jax.sharding import PartitionSpec as P

EPS = 1e-05
F32 = jnp.float32
BF16 = jnp.bfloat16
VMEM = pltpu.VMEM
SMEM = pltpu.SMEM


def params(limit=32):
    return pltpu.CompilerParams(vmem_limit_bytes=limit * 1024 * 1024)


def vspec():
    return pl.BlockSpec(memory_space=VMEM)


def tile_of(extent):
    for size in (256, 384, 128):
        if extent % size == 0:
            return size
    return extent


def live_count(count_ref):
    return count_ref[lax.axis_index("tm")]


def gather_body(count_ref, picked_ref, frames_ref, rows_ref):
    slots = picked_ref.shape[1]
    frames_dev = frames_ref.shape[0]
    live = lax.broadcasted_iota(jnp.int32, (1, slots), 1) < live_count(count_ref)
    wanted = jnp.where(live, picked_ref[...], -1).astype(F32)
    column = jnp.broadcast_to(wanted, (128, slots)).T[:, :1]
    place = lax.broadcasted_iota(jnp.int32, (1, frames_dev), 1).astype(F32)
    onehot = jnp.where(column == place, 1.0, 0.0).astype(BF16)
    rows_ref[...] = jnp.dot(onehot, frames_ref[...], preferred_element_type=F32).astype(BF16)


def gather_rows(count, picked, frames):
    slots, (frames_dev, width) = picked.shape[1], frames.shape
    return pl.pallas_call(
        gather_body,
        out_shape=jax.ShapeDtypeStruct((slots, width), BF16),
        in_specs=[pl.BlockSpec(memory_space=SMEM), vspec(), vspec()],
        out_specs=vspec(),
        compiler_params=params(),
        cost_estimate=pl.CostEstimate(
            flops=2 * slots * frames_dev * width, bytes_accessed=2 * frames_dev * width, transcendentals=0
        ),
        name="gather_rows",
    )(count, picked, frames)


def block_at(way, tensors, width):
    t, p = lax.axis_index("tensor"), lax.axis_index("pair")
    step, side = way
    index = ((t + tensors - step) % tensors) * 2 + (p + side) % 2
    return pl.multiple_of(index * width, 128)


def forward_body(ways, tensors, width, *refs):
    blocks = refs[: len(ways)]
    up_hbm, down_hbm, gain_ref, router_ref = refs[len(ways) : len(ways) + 4]
    full_ref, stats_ref, hidden_ref, slope_ref, part_ref = refs[len(ways) + 4 : len(ways) + 9]
    normed_ref, up_ref, down_ref, sems = refs[len(ways) + 9 :]
    slots, features = full_ref.shape
    hidden_dev = hidden_ref.shape[1]
    copy_up = pltpu.make_async_copy(up_hbm, up_ref, sems.at[0])
    copy_down = pltpu.make_async_copy(down_hbm, down_ref, sems.at[1])
    copy_up.start()
    copy_down.start()
    if len(ways) == 1:
        full_ref[...] = blocks[0][...]
    else:
        for way, block in zip(ways, blocks):
            full_ref[:, pl.ds(block_at(way, tensors, width), width)] = block[...]
    chunk = 32
    lane = lax.broadcasted_iota(jnp.int32, (chunk, 128), 1)

    def norm_chunk(i, _):
        rows = pl.ds(pl.multiple_of(i * chunk, chunk), chunk)
        wide = full_ref[rows, :].astype(F32)
        gate = jax.nn.sigmoid(jnp.sum(wide * router_ref[...], axis=1, keepdims=True))
        mean = jnp.sum(wide, axis=1, keepdims=True) * (1.0 / features)
        deviate = wide - mean
        inv = lax.rsqrt(jnp.sum(deviate * deviate, axis=1, keepdims=True) * (1.0 / features) + EPS)
        normed_ref[rows, :] = (deviate * inv * gain_ref[...]).astype(BF16)
        stats_ref[rows, :] = jnp.where(lane == 0, mean, jnp.where(lane == 1, inv, gate))
        return 0

    lax.fori_loop(0, slots // chunk, norm_chunk, 0)
    half_gate = 0.5 * stats_ref[:, 2:3]
    copy_up.wait()
    tile = tile_of(hidden_dev)

    def up_tile(i, _):
        cols = pl.ds(pl.multiple_of(i * tile, 128), tile)
        value = jnp.dot(normed_ref[...], up_ref[:, cols], preferred_element_type=F32)
        s = jax.nn.sigmoid(value)
        hidden_ref[:, cols] = (value * s).astype(BF16)
        slope_ref[:, cols] = half_gate * s * (1.0 + value * (1.0 - s))
        return 0

    lax.fori_loop(0, hidden_dev // tile, up_tile, 0)
    copy_down.wait()
    wide_tile = tile_of(features)

    def down_tile(i, _):
        cols = pl.ds(pl.multiple_of(i * wide_tile, 128), wide_tile)
        value = jnp.dot(hidden_ref[...], down_ref[:, cols], preferred_element_type=F32)
        part_ref[:, cols] = (value * half_gate).astype(BF16)
        return 0

    lax.fori_loop(0, features // wide_tile, down_tile, 0)


def forward(blocks, ways, tensors, up, down, gain, router):
    slots, width = blocks[0].shape
    features, hidden_dev = up.shape
    return pl.pallas_call(
        functools.partial(forward_body, ways, tensors, width),
        out_shape=(
            jax.ShapeDtypeStruct((slots, features), BF16),
            jax.ShapeDtypeStruct((slots, 128), F32),
            jax.ShapeDtypeStruct((slots, hidden_dev), BF16),
            jax.ShapeDtypeStruct((slots, hidden_dev), F32),
            jax.ShapeDtypeStruct((slots, features), BF16),
        ),
        in_specs=[vspec()] * len(blocks) + [pl.BlockSpec(memory_space=pl.ANY)] * 2 + [vspec()] * 2,
        out_specs=(vspec(),) * 5,
        scratch_shapes=[
            VMEM((slots, features), BF16),
            VMEM(up.shape, BF16),
            VMEM(down.shape, BF16),
            pltpu.SemaphoreType.DMA((2,)),
        ],
        compiler_params=params(),
        cost_estimate=pl.CostEstimate(
            flops=4 * slots * features * hidden_dev, bytes_accessed=4 * features * hidden_dev, transcendentals=0
        ),
        name="forward",
    )(*blocks, up, down, gain, router)


def backward_body(ways, tensors, width, *refs):
    blocks = refs[: len(ways)]
    up_hbm, down_hbm, gain_ref, full_ref, stats_ref, hidden_ref, slope_ref = refs[len(ways) : len(ways) + 7]
    part_ref, sums_ref = refs[len(ways) + 7 : len(ways) + 9]
    cot_ref, pre_ref, up_ref, down_ref, sems = refs[len(ways) + 9 :]
    slots, features = full_ref.shape
    hidden_dev = hidden_ref.shape[1]
    copy_up = pltpu.make_async_copy(up_hbm, up_ref, sems.at[0])
    copy_down = pltpu.make_async_copy(down_hbm, down_ref, sems.at[1])
    copy_down.start()
    copy_up.start()
    if len(ways) == 1:
        cot_ref[...] = blocks[0][...]
    else:
        for way, block in zip(ways, blocks):
            cot_ref[:, pl.ds(block_at(way, tensors, width), width)] = block[...]
    copy_down.wait()
    tile = tile_of(hidden_dev)
    over_lanes = (((1,), (1,)), ((), ()))

    def hidden_tile(i, score):
        cols = pl.ds(pl.multiple_of(i * tile, 128), tile)
        value = lax.dot_general(cot_ref[...], down_ref[cols, :], over_lanes, preferred_element_type=F32)
        pre_ref[:, cols] = (value * slope_ref[:, cols]).astype(BF16)
        return score + jnp.sum(value * hidden_ref[:, cols].astype(F32), axis=1, keepdims=True)

    score = lax.fori_loop(0, hidden_dev // tile, hidden_tile, jnp.zeros((slots, 1), F32))
    copy_up.wait()
    mean, inv = stats_ref[:, 0:1], stats_ref[:, 1:2]
    wide_tile = tile_of(features)

    def feature_tile(i, sums):
        plain, cross = sums
        cols = pl.ds(pl.multiple_of(i * wide_tile, 128), wide_tile)
        value = lax.dot_general(pre_ref[...], up_ref[cols, :], over_lanes, preferred_element_type=F32)
        scaled = value * gain_ref[:, cols]
        centred = (full_ref[:, cols].astype(F32) - mean) * inv
        part_ref[:, cols] = (scaled * inv).astype(BF16)
        return (
            plain + jnp.sum(scaled, axis=1, keepdims=True),
            cross + jnp.sum(scaled * centred, axis=1, keepdims=True),
        )

    zero = jnp.zeros((slots, 1), F32)
    plain, cross = lax.fori_loop(0, features // wide_tile, feature_tile, (zero, zero))
    lane = lax.broadcasted_iota(jnp.int32, (slots, 128), 1)
    table = jnp.where(lane == 0, plain, jnp.where(lane == 1, cross, score))
    sums_ref[...] = table.T[:8, :]


def backward(blocks, ways, tensors, up, down, gain, full, stats, hidden, slope):
    slots, width = blocks[0].shape
    features, hidden_dev = up.shape
    return pl.pallas_call(
        functools.partial(backward_body, ways, tensors, width),
        out_shape=(jax.ShapeDtypeStruct((slots, features), BF16), jax.ShapeDtypeStruct((8, slots), F32)),
        in_specs=[vspec()] * len(blocks) + [pl.BlockSpec(memory_space=pl.ANY)] * 2 + [vspec()] * 5,
        out_specs=(vspec(),) * 2,
        scratch_shapes=[
            VMEM((slots, features), BF16),
            VMEM((slots, hidden_dev), BF16),
            VMEM(up.shape, BF16),
            VMEM(down.shape, BF16),
            pltpu.SemaphoreType.DMA((2,)),
        ],
        compiler_params=params(),
        cost_estimate=pl.CostEstimate(
            flops=4 * slots * features * hidden_dev, bytes_accessed=4 * features * hidden_dev, transcendentals=0
        ),
        name="backward",
    )(*blocks, up, down, gain, full, stats, hidden, slope)


def place_rows(count_ref, picked_ref, frames_ref, rows, out_ref):
    slots = picked_ref.shape[1]
    tile = out_ref.shape[0]
    live = lax.broadcasted_iota(jnp.int32, (1, slots), 1) < live_count(count_ref)
    wanted = jnp.where(live, picked_ref[...], -1)
    place = lax.broadcasted_iota(jnp.int32, (tile, 1), 0) + pl.program_id(0) * tile
    onehot = jnp.where(wanted == place, 1.0, 0.0).astype(BF16)
    added = jnp.dot(onehot, rows, preferred_element_type=F32)
    out_ref[...] = (frames_ref[...].astype(F32) + added).astype(BF16)


def mixed_body(arrived, count_ref, picked_ref, frames_ref, keep_ref, got_ref, *refs):
    out_ref, rows_ref = refs[arrived:]

    @pl.when(pl.program_id(0) == 0)
    def _():
        total = keep_ref[...].astype(F32) + got_ref[...].astype(F32)
        for block in refs[:arrived]:
            total = total + block[...].astype(F32)
        rows_ref[...] = total.astype(BF16)

    place_rows(count_ref, picked_ref, frames_ref, rows_ref[...], out_ref)


def grads_body(
    arrived, sums_count, count_ref, picked_ref, frames_ref, keep_ref, got_ref, own_ref, stats_ref, gain_ref, router_ref, *refs
):
    blocks, sums_refs = refs[:arrived], refs[arrived : arrived + sums_count]
    out_ref, rows_ref = refs[arrived + sums_count :]

    @pl.when(pl.program_id(0) == 0)
    def _():
        slots = own_ref.shape[0]
        features = gain_ref.shape[1]
        sums = sums_refs[0][...]
        for ref in sums_refs[1:]:
            sums = sums + ref[...]
        columns = jnp.broadcast_to(sums[None], (16, 8, slots)).reshape(128, slots).T
        plain_mean = columns[:, 0:1] * (1.0 / features)
        cross_mean = columns[:, 1:2] * (1.0 / features)
        mean, inv, gate = stats_ref[:, 0:1], stats_ref[:, 1:2], stats_ref[:, 2:3]
        centred = (own_ref[...].astype(F32) - mean) * inv
        total = keep_ref[...].astype(F32) + got_ref[...].astype(F32)
        for block in blocks:
            total = total + block[...].astype(F32)
        score = 0.5 * columns[:, 2:3] * gate * (1.0 - gate)
        total = total - inv * (plain_mean + centred * cross_mean) + score * router_ref[...]
        rows_ref[...] = total.astype(BF16)

    place_rows(count_ref, picked_ref, frames_ref, rows_ref[...], out_ref)


def scatter_rows(body, name, count, picked, frames, others):
    slots, (frames_dev, width) = picked.shape[1], frames.shape
    tile = 256
    whole = [pl.BlockSpec(x.shape, lambda i: (0, 0)) for x in others]
    return pl.pallas_call(
        body,
        grid=(frames_dev // tile,),
        out_shape=jax.ShapeDtypeStruct(frames.shape, BF16),
        in_specs=[
            pl.BlockSpec(memory_space=SMEM),
            pl.BlockSpec(picked.shape, lambda i: (0, 0)),
            pl.BlockSpec((tile, width), lambda i: (i, 0)),
        ]
        + whole,
        out_specs=pl.BlockSpec((tile, width), lambda i: (i, 0)),
        scratch_shapes=[VMEM((slots, width), BF16)],
        compiler_params=params(),
        cost_estimate=pl.CostEstimate(
            flops=2 * slots * frames_dev * width, bytes_accessed=4 * frames_dev * width, transcendentals=0
        ),
        name=name,
    )(count, picked, frames, *others)


def per_device(frames, router_weight, norm_gain, up_weight, down_weight, picked_rows, picked_count, cotangent):
    width = frames.shape[1]
    features = up_weight.shape[0]
    tensors = lax.axis_size("tensor")
    t, p = lax.axis_index("tensor"), lax.axis_index("pair")
    picked = picked_rows.reshape(1, -1)
    gain, router = norm_gain.reshape(1, -1), router_weight.reshape(1, -1)
    steps = range(1, tensors)

    def shift(x, k):
        return lax.ppermute(x, "tensor", [(i, (i + k) % tensors) for i in range(tensors)])

    def swap(x):
        return lax.ppermute(x, "pair", [(0, 1), (1, 0)])

    def collect(rows):
        across = [shift(rows, k) for k in steps]
        near = [rows, swap(rows)]
        ways = [(0, 0), (0, 1)] + [(k, 0) for k in steps] + [(k, 1) for k in steps]
        blocks = near + across + [swap(x) for x in across]
        if width % 128 == 0:
            return blocks, ways
        full = jnp.zeros((rows.shape[0], features), BF16)
        for (k, side), block in zip(ways, blocks):
            start = (((t + tensors - k) % tensors) * 2 + (p + side) % 2) * width
            full = lax.dynamic_update_slice_in_dim(full, block, start, 1)
        return [full], [(0, 0)]

    def columns(part, k, side):
        start = (((t + k) % tensors) * 2 + (p + side) % 2) * width
        return lax.dynamic_slice_in_dim(part, start, width, 1)

    def reduce(part):
        sent = [columns(part, k, 0).astype(F32) + swap(columns(part, k, 1)).astype(F32) for k in steps]
        across = [shift(x.astype(BF16), k) for x, k in zip(sent, steps)]
        return columns(part, 0, 0), swap(columns(part, 0, 1)), across

    rows_in = gather_rows(picked_count, picked, frames)
    in_blocks, ways = collect(rows_in)
    rows_cot = gather_rows(picked_count, picked, cotangent)
    cot_blocks, _ = collect(rows_cot)
    full, stats, hidden, slope, out_part = forward(in_blocks, ways, tensors, up_weight, down_weight, gain, router)
    out_keep, out_got, out_across = reduce(out_part)
    grad_part, sums = backward(
        cot_blocks, ways, tensors, up_weight, down_weight, gain, full, stats, hidden, slope
    )
    sums = sums + swap(sums)
    sums_across = [shift(sums, k) for k in steps]
    grad_keep, grad_got, grad_across = reduce(grad_part)
    mixed = scatter_rows(
        functools.partial(mixed_body, len(out_across)),
        "mixed_rows",
        picked_count,
        picked,
        frames,
        [out_keep, out_got] + out_across,
    )
    router_own = lax.dynamic_slice_in_dim(router, (t * 2 + p) * width, width, 1)
    frames_grad = scatter_rows(
        functools.partial(grads_body, len(grad_across), len(sums_across) + 1),
        "grad_rows",
        picked_count,
        picked,
        cotangent,
        [grad_keep, grad_got, rows_in, stats, gain, router_own] + grad_across + [sums] + sums_across,
    )
    return (mixed, frames_grad)


def solution(mesh):
    return jax.shard_map(
        per_device,
        mesh=mesh,
        in_specs=(
            P(("group", "tm"), ("tensor", "pair")),
            P(),
            P(),
            P(None, ("tensor", "pair")),
            P(("tensor", "pair"), None),
            P(("group", "tm")),
            P("group"),
            P(("group", "tm"), ("tensor", "pair")),
        ),
        out_specs=(P(("group", "tm"), ("tensor", "pair")), P(("group", "tm"), ("tensor", "pair"))),
        check_vma=False,
    )
```

```python
import functools

import jax
import jax.numpy as jnp
from jax import lax
from jax.experimental import pallas as pl
from jax.experimental.pallas import tpu as pltpu
from jax.sharding import PartitionSpec as P

EPS = 1e-05
F32 = jnp.float32
BF16 = jnp.bfloat16
VMEM = pltpu.VMEM
ANY = pl.BlockSpec(memory_space=pl.ANY)
OVER_ROWS = (((0,), (0,)), ((), ()))
OVER_LANES = (((1,), (1,)), ((), ()))


def vspec():
    return pl.BlockSpec(memory_space=VMEM)


def call(body, name, outs, ins, specs, scratch, flops, moved, limit):
    return pl.pallas_call(
        body,
        out_shape=outs,
        in_specs=specs,
        out_specs=jax.tree.map(lambda _: vspec(), outs),
        scratch_shapes=scratch,
        compiler_params=pltpu.CompilerParams(vmem_limit_bytes=limit * 1024 * 1024),
        cost_estimate=pl.CostEstimate(flops=flops, bytes_accessed=moved, transcendentals=0),
        name=name,
    )(*ins)


def chunks_of(extent):
    size = 512 if extent % 512 == 0 else extent
    return [(start, size) for start in range(0, extent, size)]


def wanted_slots(count_ref, picked_ref):
    slots = picked_ref.shape[1]
    live = lax.broadcasted_iota(jnp.int32, (8, slots), 1) < count_ref[lax.axis_index("tm")]
    wanted = jnp.where(live, jnp.broadcast_to(picked_ref[...], (8, slots)), -1)
    swapped = pltpu.roll(wanted, slots // 2, 1)
    return jnp.where(lax.axis_index("pair") == 0, wanted, swapped)[:1]


def onehot_rows(wanted, start, size):
    place = lax.broadcasted_iota(jnp.int32, (size, 1), 0) + start
    return jnp.where(wanted == place, 1.0, 0.0).astype(BF16)


def gather_body(count_ref, picked_ref, frames_hbm, mine_ref, sib_ref, frames_ref, sems):
    cuts = chunks_of(frames_ref.shape[0])
    copies = [
        pltpu.make_async_copy(frames_hbm.at[pl.ds(a, n)], frames_ref.at[pl.ds(a, n)], sems.at[i])
        for i, (a, n) in enumerate(cuts)
    ]
    for copy in copies:
        copy.start()
    wanted = wanted_slots(count_ref, picked_ref)
    total = None
    for copy, (a, n) in zip(copies, cuts):
        onehot = onehot_rows(wanted, a, n)
        copy.wait()
        part = lax.dot_general(onehot, frames_ref[a : a + n, :], OVER_ROWS, preferred_element_type=F32)
        total = part if total is None else total + part
    half = mine_ref.shape[0]
    mine_ref[...] = total[:half].astype(BF16)
    sib_ref[...] = total[half:].astype(BF16)


def gather_rows(count, picked, frames):
    slots, (frames_dev, width) = picked.shape[1], frames.shape
    out = jax.ShapeDtypeStruct((slots // 2, width), BF16)
    return call(
        gather_body,
        "gather_rows",
        (out, out),
        (count, picked, frames),
        [pl.BlockSpec(memory_space=pltpu.SMEM), vspec(), ANY],
        [VMEM(frames.shape, BF16), pltpu.SemaphoreType.DMA((len(chunks_of(frames_dev)),))],
        2 * slots * frames_dev * width,
        2 * frames_dev * width,
        10,
    )


def scatter_body(mines, sibs, count_ref, picked_ref, frames_hbm, *refs):
    parts, (out_hbm, frames_ref, out_ref, sems) = refs[: mines + sibs], refs[mines + sibs :]
    cuts = chunks_of(frames_ref.shape[0])
    loads = [
        pltpu.make_async_copy(frames_hbm.at[pl.ds(a, n)], frames_ref.at[pl.ds(a, n)], sems.at[0, i])
        for i, (a, n) in enumerate(cuts)
    ]
    stores = [
        pltpu.make_async_copy(out_ref.at[pl.ds(a, n)], out_hbm.at[pl.ds(a, n)], sems.at[1, i])
        for i, (a, n) in enumerate(cuts)
    ]
    for load in loads:
        load.start()
    wanted = wanted_slots(count_ref, picked_ref)

    def added(blocks):
        total = blocks[0][...].astype(F32)
        for block in blocks[1:]:
            total = total + block[...].astype(F32)
        return total.astype(BF16)

    rows = jnp.concatenate([added(parts[:mines]), added(parts[mines:])], axis=0)
    for load, store, (a, n) in zip(loads, stores, cuts):
        put = jnp.dot(onehot_rows(wanted, a, n), rows, preferred_element_type=F32)
        load.wait()
        out_ref[a : a + n, :] = (frames_ref[a : a + n, :].astype(F32) + put).astype(BF16)
        store.start()
    for store in stores:
        store.wait()


def scatter_rows(name, count, picked, frames, mine_parts, sib_parts):
    slots, (frames_dev, width) = picked.shape[1], frames.shape
    parts = list(mine_parts) + list(sib_parts)
    return pl.pallas_call(
        functools.partial(scatter_body, len(mine_parts), len(sib_parts)),
        out_shape=jax.ShapeDtypeStruct(frames.shape, BF16),
        in_specs=[pl.BlockSpec(memory_space=pltpu.SMEM), vspec(), ANY] + [vspec()] * len(parts),
        out_specs=ANY,
        scratch_shapes=[
            VMEM(frames.shape, BF16),
            VMEM(frames.shape, BF16),
            pltpu.SemaphoreType.DMA((2, len(chunks_of(frames_dev)))),
        ],
        compiler_params=pltpu.CompilerParams(vmem_limit_bytes=10 * 1024 * 1024),
        cost_estimate=pl.CostEstimate(
            flops=2 * slots * frames_dev * width, bytes_accessed=4 * frames_dev * width, transcendentals=0
        ),
        name=name,
    )(count, picked, frames, *parts)


def block_start(step, side, width):
    tensors = lax.axis_size("tensor")
    chip = (lax.axis_index("tensor") + tensors + step) % tensors
    return (chip * 2 + (lax.axis_index("pair") + side) % 2) * width


def assemble(full_ref, blocks, ways, width):
    if len(ways) == 1:
        full_ref[...] = blocks[0][...]
        return
    for (step, side), block in zip(ways, blocks):
        start = pl.multiple_of(block_start(-step, side, width), 128)
        full_ref[:, pl.ds(start, width)] = block[...]


def dissect(total_ref, outs, ways, width):
    if len(ways) == 1:
        outs[0][...] = total_ref[...]
        return
    for (step, side), out in zip(ways, outs):
        start = pl.multiple_of(block_start(step, side, width), 128)
        out[...] = total_ref[:, pl.ds(start, width)]


def forward_body(ways, width, *refs):
    n = len(ways)
    blocks = refs[:n]
    up_own, up_sib, down_own, down_sib, gain_ref, router_ref = refs[n : n + 6]
    outs = refs[n + 6 : 2 * n + 6]
    full_ref, stats_ref, hidden_ref, slope_ref = refs[2 * n + 6 : 2 * n + 10]
    up0, up1, down0, down1, total_ref, sems = refs[2 * n + 10 :]
    copies = [
        pltpu.make_async_copy(src, dst, sems.at[i])
        for i, (src, dst) in enumerate([(up_own, up0), (up_sib, up1), (down_own, down0), (down_sib, down1)])
    ]
    for copy in copies:
        copy.start()
    assemble(full_ref, blocks, ways, width)
    half, features = full_ref.shape
    hidden_dev = up0.shape[1]
    wide = full_ref[...].astype(F32)
    gate = jax.nn.sigmoid(jnp.sum(wide * router_ref[...], axis=1, keepdims=True))
    mean = jnp.sum(wide, axis=1, keepdims=True) * (1.0 / features)
    deviate = wide - mean
    inv = lax.rsqrt(jnp.sum(deviate * deviate, axis=1, keepdims=True) * (1.0 / features) + EPS)
    normed = (deviate * inv * gain_ref[...]).astype(BF16)
    lane = lax.broadcasted_iota(jnp.int32, (half, 128), 1)
    stats_ref[...] = jnp.where(lane == 0, mean, jnp.where(lane == 1, inv, gate))
    half_gate = 0.5 * gate
    for i, (copy, up) in enumerate(zip(copies[:2], (up0, up1))):
        copy.wait()
        value = jnp.dot(normed, up[...], preferred_element_type=F32)
        s = jax.nn.sigmoid(value)
        cols = slice(i * hidden_dev, (i + 1) * hidden_dev)
        hidden_ref[:, cols] = (value * s).astype(BF16)
        slope_ref[:, cols] = half_gate * s * (1.0 + value * (1.0 - s))
    copies[2].wait()
    total = jnp.dot(hidden_ref[:, :hidden_dev], down0[...], preferred_element_type=F32)
    copies[3].wait()
    total = total + jnp.dot(hidden_ref[:, hidden_dev:], down1[...], preferred_element_type=F32)
    total_ref[...] = (total * half_gate).astype(BF16)
    dissect(total_ref, outs, ways, width)


def forward(blocks, ways, weights, gain, router):
    half, width = blocks[0].shape
    features, hidden_dev = weights[0].shape
    piece = jax.ShapeDtypeStruct((half, width), BF16)
    got = call(
        functools.partial(forward_body, ways, width),
        "forward",
        (piece,) * len(ways)
        + (
            jax.ShapeDtypeStruct((half, features), BF16),
            jax.ShapeDtypeStruct((half, 128), F32),
            jax.ShapeDtypeStruct((half, 2 * hidden_dev), BF16),
            jax.ShapeDtypeStruct((half, 2 * hidden_dev), F32),
        ),
        (*blocks, *weights, gain, router),
        [vspec()] * len(blocks) + [ANY] * 4 + [vspec()] * 2,
        [VMEM(w.shape, BF16) for w in weights] + [VMEM((half, features), BF16), pltpu.SemaphoreType.DMA((4,))],
        8 * half * features * hidden_dev,
        8 * features * hidden_dev,
        28,
    )
    return got[: len(ways)], got[len(ways) :]


def backward_body(ways, width, *refs):
    n = len(ways)
    blocks = refs[:n]
    up_own, up_sib, down_own, down_sib, gain_ref, router_ref = refs[n : n + 6]
    full_ref, stats_ref, hidden_ref, slope_ref = refs[n + 6 : n + 10]
    outs = refs[n + 10 : 2 * n + 10]
    up0, up1, down0, down1, cot_ref, sems = refs[2 * n + 10 :]
    copies = [
        pltpu.make_async_copy(src, dst, sems.at[i])
        for i, (src, dst) in enumerate([(down_own, down0), (down_sib, down1), (up_own, up0), (up_sib, up1)])
    ]
    for copy in copies:
        copy.start()
    assemble(cot_ref, blocks, ways, width)
    half, features = full_ref.shape
    hidden_dev = up0.shape[1]
    score, pre = 0.0, []
    for i, (copy, down) in enumerate(zip(copies[:2], (down0, down1))):
        copy.wait()
        value = lax.dot_general(cot_ref[...], down[...], OVER_LANES, preferred_element_type=F32)
        cols = slice(i * hidden_dev, (i + 1) * hidden_dev)
        pre.append((value * slope_ref[:, cols]).astype(BF16))
        score = score + jnp.sum(value * hidden_ref[:, cols].astype(F32), axis=1, keepdims=True)
    copies[2].wait()
    scaled = lax.dot_general(pre[0], up0[...], OVER_LANES, preferred_element_type=F32)
    copies[3].wait()
    scaled = scaled + lax.dot_general(pre[1], up1[...], OVER_LANES, preferred_element_type=F32)
    scaled = scaled * gain_ref[...]
    mean, inv, gate = stats_ref[:, 0:1], stats_ref[:, 1:2], stats_ref[:, 2:3]
    centred = (full_ref[...].astype(F32) - mean) * inv
    plain = jnp.sum(scaled, axis=1, keepdims=True) * (1.0 / features)
    cross = jnp.sum(scaled * centred, axis=1, keepdims=True) * (1.0 / features)
    term = 0.5 * score * gate * (1.0 - gate)
    cot_ref[...] = (inv * (scaled - plain - centred * cross) + term * router_ref[...]).astype(BF16)
    dissect(cot_ref, outs, ways, width)


def backward(blocks, ways, weights, gain, router, saved):
    half, width = blocks[0].shape
    features, hidden_dev = weights[0].shape
    return call(
        functools.partial(backward_body, ways, width),
        "backward",
        (jax.ShapeDtypeStruct((half, width), BF16),) * len(ways),
        (*blocks, *weights, gain, router, *saved),
        [vspec()] * len(blocks) + [ANY] * 4 + [vspec()] * 6,
        [VMEM(w.shape, BF16) for w in weights] + [VMEM((half, features), BF16), pltpu.SemaphoreType.DMA((4,))],
        8 * half * features * hidden_dev,
        8 * features * hidden_dev,
        28,
    )


def after(value, *others):
    return lax.optimization_barrier((value, *others))[0]


def per_device(frames, router_weight, norm_gain, up_weight, down_weight, picked_rows, picked_count, cotangent):
    width = frames.shape[1]
    features = up_weight.shape[0]
    half = picked_rows.shape[0] // 2
    tensors = lax.axis_size("tensor")
    picked = picked_rows.reshape(1, -1)
    gain, router = norm_gain.reshape(1, -1), router_weight.reshape(1, -1)
    steps = range(1, tensors)
    aligned = width % 128 == 0
    pieces = [(0, 0), (0, 1)] + [(k, 0) for k in steps] + [(k, 1) for k in steps]
    ways = pieces if aligned else [(0, 0)]

    def shift(x, k):
        return lax.ppermute(x, "tensor", [(i, (i + k) % tensors) for i in range(tensors)])

    def swap(x):
        return lax.ppermute(x, "pair", [(0, 1), (1, 0)])

    def joined(blocks):
        if aligned:
            return blocks
        full = jnp.zeros((half, features), BF16)
        for (k, side), block in zip(pieces, blocks):
            full = lax.dynamic_update_slice_in_dim(full, block, block_start(-k, side, width), 1)
        return [full]

    def cut(outs):
        if aligned:
            return outs
        return [lax.dynamic_slice_in_dim(outs[0], block_start(k, side, width), width, 1) for k, side in pieces]

    def collect(mine, sib):
        far_sib = [shift(sib, k) for k in steps]
        far_mine = [shift(after(mine, sib), k) for k in steps]
        near = swap(sib)
        return [mine, near] + far_mine + [swap(x) for x in far_sib], far_sib

    def deliver(parts):
        count = tensors - 1
        far_mine = [shift(x, k) for x, k in zip(parts[2 : 2 + count], steps)]
        through = [swap(x) for x in parts[2 + count :]]
        far_sib = [shift(x, k) for x, k in zip(through, steps)]
        return [parts[0]] + far_mine, [swap(parts[1])] + far_sib

    up_sib, down_sib = swap(up_weight), swap(down_weight)
    weights = (up_weight, up_sib, down_weight, down_sib)
    mine, sib = gather_rows(picked_count, picked, frames)
    blocks, arrived = collect(mine, sib)
    cot_mine, cot_sib = gather_rows(picked_count, picked, cotangent)
    cot_sib = after(cot_sib, *arrived)
    cot_blocks, _ = collect(cot_mine, cot_sib)
    parts, saved = forward(joined(blocks), ways, weights, gain, router)
    out_mine, out_sib = deliver(cut(parts))
    grads = backward(joined(cot_blocks), ways, weights, gain, router, saved)
    grad_mine, grad_sib = deliver(cut(grads))
    mixed = scatter_rows("mixed_rows", picked_count, picked, frames, out_mine, out_sib)
    frames_grad = scatter_rows("grad_rows", picked_count, picked, cotangent, grad_mine, grad_sib)
    return (mixed, frames_grad)


def solution(mesh):
    return jax.shard_map(
        per_device,
        mesh=mesh,
        in_specs=(
            P(("group", "tm"), ("tensor", "pair")),
            P(),
            P(),
            P(None, ("tensor", "pair")),
            P(("tensor", "pair"), None),
            P(("group", "tm")),
            P("group"),
            P(("group", "tm"), ("tensor", "pair")),
        ),
        out_specs=(P(("group", "tm"), ("tensor", "pair")), P(("group", "tm"), ("tensor", "pair"))),
        check_vma=False,
    )
```

```python
import functools

import jax
import jax.numpy as jnp
from jax import lax
from jax.experimental import pallas as pl
from jax.experimental.pallas import tpu as pltpu
from jax.sharding import PartitionSpec as P

EPS = 1e-05
F32 = jnp.float32
BF16 = jnp.bfloat16
VMEM = pltpu.VMEM
ANY = pl.BlockSpec(memory_space=pl.ANY)
OVER_ROWS = (((0,), (0,)), ((), ()))
OVER_LANES = (((1,), (1,)), ((), ()))


def vspec():
    return pl.BlockSpec(memory_space=VMEM)


def fetch(sources, targets, sems):
    copies = [pltpu.make_async_copy(s, t, sems.at[i]) for i, (s, t) in enumerate(zip(sources, targets))]
    for copy in copies:
        copy.start()
    return copies


def call_in_hbm(body, name, outs, ins, scratch, flops, moved):
    return pl.pallas_call(
        body,
        out_shape=outs,
        in_specs=[ANY] * len(ins),
        out_specs=jax.tree.map(lambda _: ANY, outs),
        scratch_shapes=scratch,
        compiler_params=pltpu.CompilerParams(vmem_limit_bytes=56 * 1024 * 1024),
        cost_estimate=pl.CostEstimate(flops=flops, bytes_accessed=moved, transcendentals=0),
        name=name,
    )(*ins)


def wanted_slots(count, picked):
    slots = picked.shape[0]
    live = lax.broadcasted_iota(jnp.int32, (8, slots), 1) < count
    wanted = jnp.where(live, jnp.broadcast_to(picked.reshape(1, slots), (8, slots)), -1)
    swapped = pltpu.roll(wanted, slots // 2, 1)
    return jnp.where(lax.axis_index("pair") == 0, wanted, swapped)[:1]


def gather_body(count_hbm, picked_hbm, frames_hbm, mine_hbm, sib_hbm, frames, picked, count, mine, sib, sems):
    slots = picked.shape[0]
    frames_dev = frames.shape[0]
    copies = fetch((frames_hbm, picked_hbm, count_hbm), (frames, picked, count), sems)
    copies[1].wait()
    copies[2].wait()
    wanted = wanted_slots(count[lax.axis_index("tm")], picked[...])
    column = jnp.broadcast_to(wanted.astype(F32), (128, slots)).T[:, :1]
    place = lax.broadcasted_iota(jnp.int32, (1, frames_dev), 1).astype(F32)
    onehot = jnp.where(column == place, 1.0, 0.0).astype(BF16)
    copies[0].wait()
    rows = jnp.dot(onehot, frames[...], preferred_element_type=F32).astype(BF16)
    half = mine.shape[0]
    mine[...] = rows[:half]
    sib[...] = rows[half:]
    for copy in fetch((mine, sib), (mine_hbm, sib_hbm), sems):
        copy.wait()


def gather_rows(count, picked, frames):
    slots, (frames_dev, width) = picked.shape[0], frames.shape
    out = jax.ShapeDtypeStruct((slots // 2, width), BF16)
    return call_in_hbm(
        gather_body,
        "gather_rows",
        (out, out),
        (count, picked, frames),
        [
            VMEM(frames.shape, BF16),
            VMEM(picked.shape, jnp.int32),
            pltpu.SMEM(count.shape, jnp.int32),
            VMEM(out.shape, BF16),
            VMEM(out.shape, BF16),
            pltpu.SemaphoreType.DMA((3,)),
        ],
        2 * slots * frames_dev * width,
        2 * frames_dev * width,
    )


def scatter_body(mines, sibs, count_ref, picked_ref, frames_ref, *refs):
    parts, (out_hbm, out_ref, sems) = refs[: mines + sibs], refs[mines + sibs :]
    wanted = wanted_slots(count_ref[lax.axis_index("tm")], picked_ref[...])

    def added(blocks):
        total = blocks[0][...].astype(F32)
        for block in blocks[1:]:
            total = total + block[...].astype(F32)
        return total.astype(BF16)

    rows = jnp.concatenate([added(parts[:mines]), added(parts[mines:])], axis=0)
    stores = []
    for i, (start, size) in enumerate(chunks_of(frames_ref.shape[0])):
        place = lax.broadcasted_iota(jnp.int32, (size, 1), 0) + start
        onehot = jnp.where(wanted == place, 1.0, 0.0).astype(BF16)
        put = jnp.dot(onehot, rows, preferred_element_type=F32)
        out_ref[start : start + size, :] = (frames_ref[start : start + size, :].astype(F32) + put).astype(BF16)
        cut = pl.ds(start, size)
        store = pltpu.make_async_copy(out_ref.at[cut], out_hbm.at[cut], sems.at[i])
        store.start()
        stores.append(store)
    for store in stores:
        store.wait()


def chunks_of(extent):
    size = 512 if extent % 512 == 0 else extent
    return [(start, size) for start in range(0, extent, size)]


def scatter_rows(name, count, picked, frames, mine_parts, sib_parts):
    slots, (frames_dev, width) = picked.shape[0], frames.shape
    parts = list(mine_parts) + list(sib_parts)
    return pl.pallas_call(
        functools.partial(scatter_body, len(mine_parts), len(sib_parts)),
        out_shape=jax.ShapeDtypeStruct(frames.shape, BF16),
        in_specs=[pl.BlockSpec(memory_space=pltpu.SMEM), vspec(), vspec()] + [vspec()] * len(parts),
        out_specs=ANY,
        scratch_shapes=[VMEM(frames.shape, BF16), pltpu.SemaphoreType.DMA((len(chunks_of(frames_dev)),))],
        compiler_params=pltpu.CompilerParams(vmem_limit_bytes=8 * 1024 * 1024),
        cost_estimate=pl.CostEstimate(
            flops=2 * slots * frames_dev * width, bytes_accessed=4 * frames_dev * width, transcendentals=0
        ),
        name=name,
    )(count, picked, frames, *parts)


def block_start(step, side, width):
    tensors = lax.axis_size("tensor")
    chip = (lax.axis_index("tensor") + tensors + step) % tensors
    return (chip * 2 + (lax.axis_index("pair") + side) % 2) * width


def places(full, ways, width):
    if len(ways) == 1:
        return [full]
    return [full.at[:, pl.ds(pl.multiple_of(block_start(-k, side, width), 128), width)] for k, side in ways]


def pieces_of(total, ways, width):
    if len(ways) == 1:
        return [total]
    return [total.at[:, pl.ds(pl.multiple_of(block_start(k, side, width), 128), width)] for k, side in ways]


def forward_body(ways, width, *refs):
    n = len(ways)
    blocks, weights = refs[:n], refs[n : n + 4]
    gain_hbm, router_hbm = refs[n + 4 : n + 6]
    outs, saved = refs[n + 6 : 2 * n + 6], refs[2 * n + 6 : 2 * n + 10]
    full, gain, router, stats, hidden, slope, total, up0, up1, down0, down1, in_sems, out_sems = refs[2 * n + 10 :]
    copies = fetch(
        (*blocks, gain_hbm, router_hbm, *weights),
        (*places(full, ways, width), gain, router, up0, up1, down0, down1),
        in_sems,
    )
    half, features = full.shape
    hidden_dev = up0.shape[1]
    for copy in copies[: n + 2]:
        copy.wait()
    wide = full[...].astype(F32)
    gate = jax.nn.sigmoid(jnp.sum(wide * router[...].reshape(1, features), axis=1, keepdims=True))
    mean = jnp.sum(wide, axis=1, keepdims=True) * (1.0 / features)
    deviate = wide - mean
    inv = lax.rsqrt(jnp.sum(deviate * deviate, axis=1, keepdims=True) * (1.0 / features) + EPS)
    normed = (deviate * inv * gain[...].reshape(1, features)).astype(BF16)
    lane = lax.broadcasted_iota(jnp.int32, (half, 128), 1)
    stats[...] = jnp.where(lane == 0, mean, jnp.where(lane == 1, inv, gate))
    half_gate = 0.5 * gate
    for i, (copy, up) in enumerate(zip(copies[n + 2 : n + 4], (up0, up1))):
        copy.wait()
        value = jnp.dot(normed, up[...], preferred_element_type=F32)
        s = jax.nn.sigmoid(value)
        cols = slice(i * hidden_dev, (i + 1) * hidden_dev)
        hidden[:, cols] = (value * s).astype(BF16)
        slope[:, cols] = half_gate * s * (1.0 + value * (1.0 - s))
    saving = fetch((full, stats, hidden, slope), saved, out_sems)
    copies[n + 4].wait()
    value = jnp.dot(hidden[:, :hidden_dev], down0[...], preferred_element_type=F32)
    copies[n + 5].wait()
    value = value + jnp.dot(hidden[:, hidden_dev:], down1[...], preferred_element_type=F32)
    total[...] = (value * half_gate).astype(BF16)
    for copy in fetch(pieces_of(total, ways, width), outs, in_sems) + saving:
        copy.wait()


def forward(blocks, ways, weights, gain, router):
    half, block = blocks[0].shape
    features, hidden_dev = weights[0].shape
    saved = (
        ((half, features), BF16),
        ((half, 128), F32),
        ((half, 2 * hidden_dev), BF16),
        ((half, 2 * hidden_dev), F32),
    )
    got = call_in_hbm(
        functools.partial(forward_body, ways, block),
        "forward",
        (jax.ShapeDtypeStruct((half, block), BF16),) * len(ways) + tuple(jax.ShapeDtypeStruct(*x) for x in saved),
        (*blocks, *weights, gain, router),
        [
            VMEM(*saved[0]),
            VMEM(gain.shape, F32),
            VMEM(router.shape, F32),
            *[VMEM(*x) for x in saved[1:]],
            VMEM(*saved[0]),
            *[VMEM(w.shape, BF16) for w in weights],
            pltpu.SemaphoreType.DMA((len(ways) + 6,)),
            pltpu.SemaphoreType.DMA((4,)),
        ],
        8 * half * features * hidden_dev,
        8 * features * hidden_dev,
    )
    return got[: len(ways)], got[len(ways) :]


def backward_body(ways, width, *refs):
    n = len(ways)
    blocks, (up_own, up_sib, down_own, down_sib) = refs[:n], refs[n : n + 4]
    smalls, saved, outs = refs[n + 4 : n + 6], refs[n + 6 : n + 10], refs[n + 10 : 2 * n + 10]
    cot, gain, router, full, stats, hidden, slope, up0, up1, down0, down1, sems = refs[2 * n + 10 :]
    copies = fetch(
        (*blocks, down_own, saved[2], saved[3], down_sib, up_own, up_sib, *smalls, saved[0], saved[1]),
        (*places(cot, ways, width), down0, hidden, slope, down1, up0, up1, gain, router, full, stats),
        sems,
    )
    half, features = full.shape
    hidden_dev = up0.shape[1]
    for copy in copies[: n + 3]:
        copy.wait()
    score, pre = 0.0, []
    for i, down in enumerate((down0, down1)):
        if i:
            copies[n + 3].wait()
        value = lax.dot_general(cot[...], down[...], OVER_LANES, preferred_element_type=F32)
        cols = slice(i * hidden_dev, (i + 1) * hidden_dev)
        pre.append((value * slope[:, cols]).astype(BF16))
        score = score + jnp.sum(value * hidden[:, cols].astype(F32), axis=1, keepdims=True)
    copies[n + 4].wait()
    scaled = lax.dot_general(pre[0], up0[...], OVER_LANES, preferred_element_type=F32)
    copies[n + 5].wait()
    scaled = scaled + lax.dot_general(pre[1], up1[...], OVER_LANES, preferred_element_type=F32)
    for copy in copies[n + 6 :]:
        copy.wait()
    scaled = scaled * gain[...].reshape(1, features)
    mean, inv, gate = stats[:, 0:1], stats[:, 1:2], stats[:, 2:3]
    centred = (full[...].astype(F32) - mean) * inv
    plain = jnp.sum(scaled, axis=1, keepdims=True) * (1.0 / features)
    cross = jnp.sum(scaled * centred, axis=1, keepdims=True) * (1.0 / features)
    term = 0.5 * score * gate * (1.0 - gate)
    cot[...] = (inv * (scaled - plain - centred * cross) + term * router[...].reshape(1, features)).astype(BF16)
    for copy in fetch(pieces_of(cot, ways, width), outs, sems):
        copy.wait()


def backward(blocks, ways, weights, gain, router, saved):
    half, block = blocks[0].shape
    features, hidden_dev = weights[0].shape
    return call_in_hbm(
        functools.partial(backward_body, ways, block),
        "backward",
        (jax.ShapeDtypeStruct((half, block), BF16),) * len(ways),
        (*blocks, *weights, gain, router, *saved),
        [
            VMEM((half, features), BF16),
            VMEM(gain.shape, F32),
            VMEM(router.shape, F32),
            *[VMEM(x.shape, x.dtype) for x in saved],
            *[VMEM(w.shape, BF16) for w in weights],
            pltpu.SemaphoreType.DMA((len(ways) + 10,)),
        ],
        8 * half * features * hidden_dev,
        8 * features * hidden_dev,
    )


def after(value, *others):
    return lax.optimization_barrier((value, *others))[0]


def per_device(frames, router_weight, norm_gain, up_weight, down_weight, picked_rows, picked_count, cotangent):
    width = frames.shape[1]
    features = up_weight.shape[0]
    half = picked_rows.shape[0] // 2
    tensors = lax.axis_size("tensor")
    picked, gain, router = picked_rows, norm_gain, router_weight
    steps = range(1, tensors)
    aligned = width % 128 == 0
    pieces = [(0, 0), (0, 1)] + [(k, 0) for k in steps] + [(k, 1) for k in steps]
    ways = pieces if aligned else [(0, 0)]

    def shift(x, k):
        return lax.ppermute(x, "tensor", [(i, (i + k) % tensors) for i in range(tensors)])

    def swap(x):
        return lax.ppermute(x, "pair", [(0, 1), (1, 0)])

    def joined(blocks):
        if aligned:
            return blocks
        full = jnp.zeros((half, features), BF16)
        for (k, side), block in zip(pieces, blocks):
            full = lax.dynamic_update_slice_in_dim(full, block, block_start(-k, side, width), 1)
        return [full]

    def cut(outs):
        if aligned:
            return outs
        return [lax.dynamic_slice_in_dim(outs[0], block_start(k, side, width), width, 1) for k, side in pieces]

    def collect(mine, sib):
        far_sib = [shift(sib, k) for k in steps]
        far_mine = [shift(after(mine, sib), k) for k in steps]
        near = swap(sib)
        return [mine, near] + far_mine + [swap(x) for x in far_sib], far_sib

    def deliver(parts):
        count = tensors - 1
        far_mine = [shift(x, k) for x, k in zip(parts[2 : 2 + count], steps)]
        through = [swap(x) for x in parts[2 + count :]]
        far_sib = [shift(x, k) for x, k in zip(through, steps)]
        return [parts[0]] + far_mine, [swap(parts[1])] + far_sib, through

    up_sib, down_sib = swap(up_weight), swap(down_weight)
    weights = (up_weight, up_sib, down_weight, down_sib)
    mine, sib = gather_rows(picked_count, picked, frames)
    blocks, arrived = collect(mine, sib)
    cot_mine, cot_sib = gather_rows(picked_count, picked, cotangent)
    cot_sib = after(cot_sib, *arrived)
    cot_blocks, _ = collect(cot_mine, cot_sib)
    parts, saved = forward(joined(blocks), ways, weights, gain, router)
    out_mine, out_sib, through = deliver(cut(parts))
    cot_full = joined(cot_blocks)
    cot_full[0] = after(cot_full[0], *through)
    grads = backward(cot_full, ways, weights, gain, router, saved)
    grad_mine, grad_sib, _ = deliver(cut(grads))
    mixed = scatter_rows("mixed_rows", picked_count, picked, frames, out_mine, out_sib)
    grad_mine[0] = after(grad_mine[0], mixed)
    frames_grad = scatter_rows("grad_rows", picked_count, picked, cotangent, grad_mine, grad_sib)
    return (mixed, frames_grad)


def solution(mesh):
    return jax.shard_map(
        per_device,
        mesh=mesh,
        in_specs=(
            P(("group", "tm"), ("tensor", "pair")),
            P(),
            P(),
            P(None, ("tensor", "pair")),
            P(("tensor", "pair"), None),
            P(("group", "tm")),
            P("group"),
            P(("group", "tm"), ("tensor", "pair")),
        ),
        out_specs=(P(("group", "tm"), ("tensor", "pair")), P(("group", "tm"), ("tensor", "pair"))),
        check_vma=False,
    )
```

```python
import functools

import jax
import jax.numpy as jnp
from jax import lax
from jax.experimental import pallas as pl
from jax.experimental.pallas import tpu as pltpu
from jax.sharding import PartitionSpec as P

EPS = 1e-05
F32 = jnp.float32
BF16 = jnp.bfloat16
VMEM = pltpu.VMEM
ANY = pl.BlockSpec(memory_space=pl.ANY)
OVER_LANES = (((1,), (1,)), ((), ()))


def vspec():
    return pl.BlockSpec(memory_space=VMEM)


def call(body, name, outs, ins, specs, scratch, flops, moved, limit):
    return pl.pallas_call(
        body,
        out_shape=outs,
        in_specs=specs,
        out_specs=jax.tree.map(lambda _: vspec(), outs),
        scratch_shapes=scratch,
        compiler_params=pltpu.CompilerParams(vmem_limit_bytes=limit * 1024 * 1024),
        cost_estimate=pl.CostEstimate(flops=flops, bytes_accessed=moved, transcendentals=0),
        name=name,
    )(*ins)


def chunks_of(extent):
    size = 512 if extent % 512 == 0 else extent
    return [(start, size) for start in range(0, extent, size)]


def fetch(sources, targets, sems):
    copies = [pltpu.make_async_copy(s, t, sems.at[i]) for i, (s, t) in enumerate(zip(sources, targets))]
    for copy in copies:
        copy.start()
    return copies


def call_in_hbm(body, name, outs, ins, scratch, flops, moved):
    return pl.pallas_call(
        body,
        out_shape=outs,
        in_specs=[ANY] * len(ins),
        out_specs=jax.tree.map(lambda _: ANY, outs),
        scratch_shapes=scratch,
        compiler_params=pltpu.CompilerParams(vmem_limit_bytes=56 * 1024 * 1024),
        cost_estimate=pl.CostEstimate(flops=flops, bytes_accessed=moved, transcendentals=0),
        name=name,
    )(*ins)


def wanted_slots(count, picked):
    slots = picked.shape[0]
    live = lax.broadcasted_iota(jnp.int32, (8, slots), 1) < count
    wanted = jnp.where(live, jnp.broadcast_to(picked.reshape(1, slots), (8, slots)), -1)
    swapped = pltpu.roll(wanted, slots // 2, 1)
    return jnp.where(lax.axis_index("pair") == 0, wanted, swapped)[:1]


def gather_body(count_hbm, picked_hbm, frames_hbm, mine_hbm, sib_hbm, wanted_hbm, frames, picked, count, mine, sib, sems):
    slots = picked.shape[0]
    frames_dev = frames.shape[0]
    copies = fetch((frames_hbm, picked_hbm, count_hbm), (frames, picked, count), sems)
    copies[1].wait()
    copies[2].wait()
    wanted = wanted_slots(count[lax.axis_index("tm")], picked[...])
    picked[...] = wanted.reshape(slots)
    column = jnp.broadcast_to(wanted.astype(F32), (128, slots)).T[:, :1]
    place = lax.broadcasted_iota(jnp.int32, (1, frames_dev), 1).astype(F32)
    onehot = jnp.where(column == place, 1.0, 0.0).astype(BF16)
    copies[0].wait()
    rows = jnp.dot(onehot, frames[...], preferred_element_type=F32).astype(BF16)
    half = mine.shape[0]
    mine[...] = rows[:half]
    sib[...] = rows[half:]
    for copy in fetch((sib, mine, picked), (sib_hbm, mine_hbm, wanted_hbm), sems):
        copy.wait()


def gather_rows(count, picked, frames, moved):
    slots, (frames_dev, width) = picked.shape[0], frames.shape
    out = jax.ShapeDtypeStruct((slots // 2, width), BF16)
    return call_in_hbm(
        gather_body,
        "gather_rows",
        (out, out, jax.ShapeDtypeStruct(picked.shape, jnp.int32)),
        (count, picked, frames),
        [
            VMEM(frames.shape, BF16),
            VMEM(picked.shape, jnp.int32),
            pltpu.SMEM(count.shape, jnp.int32),
            VMEM(out.shape, BF16),
            VMEM(out.shape, BF16),
            pltpu.SemaphoreType.DMA((3,)),
        ],
        2 * slots * frames_dev * width,
        moved,
    )


def scatter_body(mines, sibs, wanted_ref, frames_ref, *refs):
    parts, (out_hbm, out_ref, sems) = refs[: mines + sibs], refs[mines + sibs :]
    wanted = wanted_ref[...].reshape(1, wanted_ref.shape[0])

    def added(blocks):
        total = blocks[0][...].astype(F32)
        for block in blocks[1:]:
            total = total + block[...].astype(F32)
        return total.astype(BF16)

    rows = jnp.concatenate([added(parts[:mines]), added(parts[mines:])], axis=0)
    stores = []
    for i, (start, size) in enumerate(chunks_of(frames_ref.shape[0])):
        place = lax.broadcasted_iota(jnp.int32, (size, 1), 0) + start
        onehot = jnp.where(wanted == place, 1.0, 0.0).astype(BF16)
        put = jnp.dot(onehot, rows, preferred_element_type=F32)
        out_ref[start : start + size, :] = (frames_ref[start : start + size, :].astype(F32) + put).astype(BF16)
        cut = pl.ds(start, size)
        store = pltpu.make_async_copy(out_ref.at[cut], out_hbm.at[cut], sems.at[i])
        store.start()
        stores.append(store)
    for store in stores:
        store.wait()


def scatter_rows(name, wanted, frames, mine_parts, sib_parts):
    slots, (frames_dev, width) = wanted.shape[0], frames.shape
    parts = list(mine_parts) + list(sib_parts)
    return pl.pallas_call(
        functools.partial(scatter_body, len(mine_parts), len(sib_parts)),
        out_shape=jax.ShapeDtypeStruct(frames.shape, BF16),
        in_specs=[vspec(), vspec()] + [vspec()] * len(parts),
        out_specs=ANY,
        scratch_shapes=[VMEM(frames.shape, BF16), pltpu.SemaphoreType.DMA((len(chunks_of(frames_dev)),))],
        compiler_params=pltpu.CompilerParams(vmem_limit_bytes=8 * 1024 * 1024),
        cost_estimate=pl.CostEstimate(
            flops=2 * slots * frames_dev * width, bytes_accessed=4 * frames_dev * width, transcendentals=0
        ),
        name=name,
    )(wanted, frames, *parts)


def block_start(step, side, width):
    tensors = lax.axis_size("tensor")
    chip = (lax.axis_index("tensor") + tensors + step) % tensors
    return (chip * 2 + (lax.axis_index("pair") + side) % 2) * width


def assemble(full_ref, blocks, ways, width):
    if len(ways) == 1:
        full_ref[...] = blocks[0][...]
        return
    for (step, side), block in zip(ways, blocks):
        start = pl.multiple_of(block_start(-step, side, width), 128)
        full_ref[:, pl.ds(start, width)] = block[...]


def dissect(total_ref, outs, ways, width):
    if len(ways) == 1:
        outs[0][...] = total_ref[...]
        return
    for (step, side), out in zip(ways, outs):
        start = pl.multiple_of(block_start(step, side, width), 128)
        out[...] = total_ref[:, pl.ds(start, width)]


def forward_body(ways, width, *refs):
    n = len(ways)
    blocks = refs[:n]
    up_own, up_sib, down_own, down_sib, gain_ref, router_ref = refs[n : n + 6]
    outs = refs[n + 6 : 2 * n + 6]
    full_ref, stats_ref, hidden_ref, slope_ref = refs[2 * n + 6 : 2 * n + 10]
    (total_ref,) = refs[2 * n + 10 :]
    assemble(full_ref, blocks, ways, width)
    half, features = full_ref.shape
    hidden_dev = up_own.shape[1]
    wide = full_ref[...].astype(F32)
    gate = jax.nn.sigmoid(jnp.sum(wide * router_ref[...].reshape(1, features), axis=1, keepdims=True))
    mean = jnp.sum(wide, axis=1, keepdims=True) * (1.0 / features)
    deviate = wide - mean
    inv = lax.rsqrt(jnp.sum(deviate * deviate, axis=1, keepdims=True) * (1.0 / features) + EPS)
    normed = (deviate * inv * gain_ref[...].reshape(1, features)).astype(BF16)
    lane = lax.broadcasted_iota(jnp.int32, (half, 128), 1)
    stats_ref[...] = jnp.where(lane == 0, mean, jnp.where(lane == 1, inv, gate))
    half_gate = 0.5 * gate
    for i, up in enumerate((up_own, up_sib)):
        value = jnp.dot(normed, up[...], preferred_element_type=F32)
        s = jax.nn.sigmoid(value)
        cols = slice(i * hidden_dev, (i + 1) * hidden_dev)
        hidden_ref[:, cols] = (value * s).astype(BF16)
        slope_ref[:, cols] = half_gate * s * (1.0 + value * (1.0 - s))
    total = jnp.dot(hidden_ref[:, :hidden_dev], down_own[...], preferred_element_type=F32)
    total = total + jnp.dot(hidden_ref[:, hidden_dev:], down_sib[...], preferred_element_type=F32)
    total_ref[...] = (total * half_gate).astype(BF16)
    dissect(total_ref, outs, ways, width)


def forward(blocks, ways, weights, gain, router):
    half, width = blocks[0].shape
    features, hidden_dev = weights[0].shape
    piece = jax.ShapeDtypeStruct((half, width), BF16)
    got = call(
        functools.partial(forward_body, ways, width),
        "forward",
        (piece,) * len(ways)
        + (
            jax.ShapeDtypeStruct((half, features), BF16),
            jax.ShapeDtypeStruct((half, 128), F32),
            jax.ShapeDtypeStruct((half, 2 * hidden_dev), BF16),
            jax.ShapeDtypeStruct((half, 2 * hidden_dev), F32),
        ),
        (*blocks, *weights, gain, router),
        [vspec()] * (len(blocks) + 6),
        [VMEM((half, features), BF16)],
        1,
        1,
        16,
    )
    return got[: len(ways)], got[len(ways) :]


def backward_body(ways, width, *refs):
    n = len(ways)
    blocks = refs[:n]
    up_own, up_sib, down_own, down_sib, gain_ref, router_ref = refs[n : n + 6]
    full_ref, stats_ref, hidden_ref, slope_ref = refs[n + 6 : n + 10]
    outs = refs[n + 10 : 2 * n + 10]
    (cot_ref,) = refs[2 * n + 10 :]
    assemble(cot_ref, blocks, ways, width)
    half, features = full_ref.shape
    hidden_dev = up_own.shape[1]
    score, pre = 0.0, []
    for i, down in enumerate((down_own, down_sib)):
        value = lax.dot_general(cot_ref[...], down[...], OVER_LANES, preferred_element_type=F32)
        cols = slice(i * hidden_dev, (i + 1) * hidden_dev)
        pre.append((value * slope_ref[:, cols]).astype(BF16))
        score = score + jnp.sum(value * hidden_ref[:, cols].astype(F32), axis=1, keepdims=True)
    scaled = lax.dot_general(pre[0], up_own[...], OVER_LANES, preferred_element_type=F32)
    scaled = scaled + lax.dot_general(pre[1], up_sib[...], OVER_LANES, preferred_element_type=F32)
    scaled = scaled * gain_ref[...].reshape(1, features)
    mean, inv, gate = stats_ref[:, 0:1], stats_ref[:, 1:2], stats_ref[:, 2:3]
    centred = (full_ref[...].astype(F32) - mean) * inv
    plain = jnp.sum(scaled, axis=1, keepdims=True) * (1.0 / features)
    cross = jnp.sum(scaled * centred, axis=1, keepdims=True) * (1.0 / features)
    term = 0.5 * score * gate * (1.0 - gate)
    cot_ref[...] = (inv * (scaled - plain - centred * cross) + term * router_ref[...].reshape(1, features)).astype(BF16)
    dissect(cot_ref, outs, ways, width)


def backward(blocks, ways, weights, gain, router, saved):
    half, width = blocks[0].shape
    features, hidden_dev = weights[0].shape
    return call(
        functools.partial(backward_body, ways, width),
        "backward",
        (jax.ShapeDtypeStruct((half, width), BF16),) * len(ways),
        (*blocks, *weights, gain, router, *saved),
        [vspec()] * (len(blocks) + 10),
        [VMEM((half, features), BF16)],
        1,
        1,
        16,
    )


def after(value, *others):
    return lax.optimization_barrier((value, *others))[0]


def per_device(frames, router_weight, norm_gain, up_weight, down_weight, picked_rows, picked_count, cotangent):
    width = frames.shape[1]
    features = up_weight.shape[0]
    half = picked_rows.shape[0] // 2
    tensors = lax.axis_size("tensor")
    gain, router = norm_gain, router_weight
    steps = range(1, tensors)
    aligned = width % 128 == 0
    pieces = [(0, 0), (0, 1)] + [(k, 0) for k in steps] + [(k, 1) for k in steps]
    ways = pieces if aligned else [(0, 0)]

    def send(x, k, side):
        pairs = [
            (chip * 2 + core, (chip + k) % tensors * 2 + (core + side) % 2) for chip in range(tensors) for core in (0, 1)
        ]
        return lax.ppermute(x, ("tensor", "pair"), pairs)

    def swap(x):
        return lax.ppermute(x, "pair", [(0, 1), (1, 0)])

    def joined(blocks):
        if aligned:
            return blocks
        full = jnp.zeros((half, features), BF16)
        for (k, side), block in zip(pieces, blocks):
            full = lax.dynamic_update_slice_in_dim(full, block, block_start(-k, side, width), 1)
        return [full]

    def cut(outs):
        if aligned:
            return outs
        return [lax.dynamic_slice_in_dim(outs[0], block_start(k, side, width), width, 1) for k, side in pieces]

    def collect(mine, sib):
        return [mine, swap(sib)] + [send(mine, k, 0) for k in steps] + [send(sib, k, 1) for k in steps]

    def deliver(parts):
        count = tensors - 1
        far_mine = [send(x, k, 0) for x, k in zip(parts[2 : 2 + count], steps)]
        far_sib = [send(x, k, 1) for x, k in zip(parts[2 + count :], steps)]
        return [parts[0]] + far_mine, [swap(parts[1])] + far_sib

    up_sib, down_sib = swap(up_weight), swap(down_weight)
    weights = (up_weight, up_sib, down_weight, down_sib)
    mine, sib, wanted = gather_rows(picked_count, picked_rows, frames, 1)
    blocks = collect(mine, sib)
    cot_mine, cot_sib, _ = gather_rows(picked_count, picked_rows, cotangent, 1)
    cot_mine, cot_sib = lax.optimization_barrier((cot_mine, cot_sib, blocks[2]))[:2]
    cot_blocks = collect(cot_mine, cot_sib)
    parts, saved = forward(joined(blocks), ways, weights, gain, router)
    out_mine, out_sib = deliver(cut(parts))
    grads = backward(joined(cot_blocks), ways, weights, gain, router, saved)
    grad_mine, grad_sib = deliver(cut(grads))
    mixed = scatter_rows("mixed_rows", wanted, frames, out_mine, out_sib)
    grad_mine[0] = after(grad_mine[0], mixed)
    frames_grad = scatter_rows("grad_rows", wanted, cotangent, grad_mine, grad_sib)
    return (mixed, frames_grad)


def solution(mesh):
    return jax.shard_map(
        per_device,
        mesh=mesh,
        in_specs=(
            P(("group", "tm"), ("tensor", "pair")),
            P(),
            P(),
            P(None, ("tensor", "pair")),
            P(("tensor", "pair"), None),
            P(("group", "tm")),
            P("group"),
            P(("group", "tm"), ("tensor", "pair")),
        ),
        out_specs=(P(("group", "tm"), ("tensor", "pair")), P(("group", "tm"), ("tensor", "pair"))),
        check_vma=False,
    )
```

```python
import functools

import jax
import jax.numpy as jnp
from jax import lax
from jax.experimental import pallas as pl
from jax.experimental.pallas import tpu as pltpu
from jax.sharding import PartitionSpec as P

EPS = 1e-05
F32 = jnp.float32
BF16 = jnp.bfloat16
VMEM = pltpu.VMEM
ANY = pl.BlockSpec(memory_space=pl.ANY)
OVER_LANES = (((1,), (1,)), ((), ()))


def vspec():
    return pl.BlockSpec(memory_space=VMEM)


def call(body, name, outs, ins, specs, scratch, flops, moved, limit):
    return pl.pallas_call(
        body,
        out_shape=outs,
        in_specs=specs,
        out_specs=jax.tree.map(lambda _: vspec(), outs),
        scratch_shapes=scratch,
        compiler_params=pltpu.CompilerParams(vmem_limit_bytes=limit * 1024 * 1024),
        cost_estimate=pl.CostEstimate(flops=flops, bytes_accessed=moved, transcendentals=0),
        name=name,
    )(*ins)


def chunks_of(extent):
    size = 512 if extent % 512 == 0 else extent
    return [(start, size) for start in range(0, extent, size)]


def fetch(sources, targets, sems):
    copies = [pltpu.make_async_copy(s, t, sems.at[i]) for i, (s, t) in enumerate(zip(sources, targets))]
    for copy in copies:
        copy.start()
    return copies


def call_in_hbm(body, name, outs, ins, scratch, flops, moved):
    return pl.pallas_call(
        body,
        out_shape=outs,
        in_specs=[ANY] * len(ins),
        out_specs=jax.tree.map(lambda _: ANY, outs),
        scratch_shapes=scratch,
        compiler_params=pltpu.CompilerParams(vmem_limit_bytes=56 * 1024 * 1024),
        cost_estimate=pl.CostEstimate(flops=flops, bytes_accessed=moved, transcendentals=0),
        name=name,
    )(*ins)


def wanted_slots(count, picked):
    slots = picked.shape[0]
    live = lax.broadcasted_iota(jnp.int32, (8, slots), 1) < count
    wanted = jnp.where(live, jnp.broadcast_to(picked.reshape(1, slots), (8, slots)), -1)
    swapped = pltpu.roll(wanted, slots // 2, 1)
    return jnp.where(lax.axis_index("pair") == 0, wanted, swapped)[:1]


def gather_body(count_hbm, picked_hbm, frames_hbm, mine_hbm, sib_hbm, wanted_hbm, frames, picked, count, mine, sib, sems):
    slots = picked.shape[0]
    frames_dev = frames.shape[0]
    copies = fetch((frames_hbm, picked_hbm, count_hbm), (frames, picked, count), sems)
    copies[1].wait()
    copies[2].wait()
    wanted = wanted_slots(count[lax.axis_index("tm")], picked[...])
    picked[...] = wanted.reshape(slots)
    column = jnp.broadcast_to(wanted.astype(F32), (128, slots)).T[:, :1]
    place = lax.broadcasted_iota(jnp.int32, (1, frames_dev), 1).astype(F32)
    onehot = jnp.where(column == place, 1.0, 0.0).astype(BF16)
    copies[0].wait()
    rows = jnp.dot(onehot, frames[...], preferred_element_type=F32).astype(BF16)
    half = mine.shape[0]
    mine[...] = rows[:half]
    sib[...] = rows[half:]
    for copy in fetch((sib, mine, picked), (sib_hbm, mine_hbm, wanted_hbm), sems):
        copy.wait()


def gather_rows(count, picked, frames, moved):
    slots, (frames_dev, width) = picked.shape[0], frames.shape
    out = jax.ShapeDtypeStruct((slots // 2, width), BF16)
    return call_in_hbm(
        gather_body,
        "gather_rows",
        (out, out, jax.ShapeDtypeStruct(picked.shape, jnp.int32)),
        (count, picked, frames),
        [
            VMEM(frames.shape, BF16),
            VMEM(picked.shape, jnp.int32),
            pltpu.SMEM(count.shape, jnp.int32),
            VMEM(out.shape, BF16),
            VMEM(out.shape, BF16),
            pltpu.SemaphoreType.DMA((3,)),
        ],
        2 * slots * frames_dev * width,
        moved,
    )


def scatter_body(mines, sibs, wanted_ref, frames_ref, *refs):
    parts, (out_hbm, out_ref, sems) = refs[: mines + sibs], refs[mines + sibs :]
    wanted = wanted_ref[...].reshape(1, wanted_ref.shape[0])

    def added(blocks):
        total = blocks[0][...].astype(F32)
        for block in blocks[1:]:
            total = total + block[...].astype(F32)
        return total.astype(BF16)

    rows = jnp.concatenate([added(parts[:mines]), added(parts[mines:])], axis=0)
    stores = []
    for i, (start, size) in enumerate(chunks_of(frames_ref.shape[0])):
        place = lax.broadcasted_iota(jnp.int32, (size, 1), 0) + start
        onehot = jnp.where(wanted == place, 1.0, 0.0).astype(BF16)
        put = jnp.dot(onehot, rows, preferred_element_type=F32)
        out_ref[start : start + size, :] = (frames_ref[start : start + size, :].astype(F32) + put).astype(BF16)
        cut = pl.ds(start, size)
        store = pltpu.make_async_copy(out_ref.at[cut], out_hbm.at[cut], sems.at[i])
        store.start()
        stores.append(store)
    for store in stores:
        store.wait()


def scatter_rows(name, wanted, frames, mine_parts, sib_parts):
    slots, (frames_dev, width) = wanted.shape[0], frames.shape
    parts = list(mine_parts) + list(sib_parts)
    return pl.pallas_call(
        functools.partial(scatter_body, len(mine_parts), len(sib_parts)),
        out_shape=jax.ShapeDtypeStruct(frames.shape, BF16),
        in_specs=[vspec(), vspec()] + [vspec()] * len(parts),
        out_specs=ANY,
        scratch_shapes=[VMEM(frames.shape, BF16), pltpu.SemaphoreType.DMA((len(chunks_of(frames_dev)),))],
        compiler_params=pltpu.CompilerParams(vmem_limit_bytes=8 * 1024 * 1024),
        cost_estimate=pl.CostEstimate(
            flops=2 * slots * frames_dev * width, bytes_accessed=4 * frames_dev * width, transcendentals=0
        ),
        name=name,
    )(wanted, frames, *parts)


def block_start(step, side, width):
    tensors = lax.axis_size("tensor")
    chip = (lax.axis_index("tensor") + tensors + step) % tensors
    return (chip * 2 + (lax.axis_index("pair") + side) % 2) * width


def assemble(full_ref, blocks, ways, width):
    if len(ways) == 1:
        full_ref[...] = blocks[0][...]
        return
    for (step, side), block in zip(ways, blocks):
        start = pl.multiple_of(block_start(-step, side, width), 128)
        full_ref[:, pl.ds(start, width)] = block[...]


def dissect(total_ref, outs, ways, width):
    if len(ways) == 1:
        outs[0][...] = total_ref[...]
        return
    for (step, side), out in zip(ways, outs):
        start = pl.multiple_of(block_start(step, side, width), 128)
        out[...] = total_ref[:, pl.ds(start, width)]


def forward_body(ways, width, *refs):
    n = len(ways)
    blocks = refs[:n]
    up_own, up_sib, down_own, down_sib, gain_ref, router_ref = refs[n : n + 6]
    outs = refs[n + 6 : 2 * n + 6]
    full_ref, stats_ref, hidden_ref, slope_ref = refs[2 * n + 6 : 2 * n + 10]
    (total_ref,) = refs[2 * n + 10 :]
    assemble(full_ref, blocks, ways, width)
    half, features = full_ref.shape
    hidden_dev = up_own.shape[1]
    wide = full_ref[...].astype(F32)
    gate = jax.nn.sigmoid(jnp.sum(wide * router_ref[...].reshape(1, features), axis=1, keepdims=True))
    mean = jnp.sum(wide, axis=1, keepdims=True) * (1.0 / features)
    deviate = wide - mean
    inv = lax.rsqrt(jnp.sum(deviate * deviate, axis=1, keepdims=True) * (1.0 / features) + EPS)
    normed = (deviate * inv * gain_ref[...].reshape(1, features)).astype(BF16)
    lane = lax.broadcasted_iota(jnp.int32, (half, 128), 1)
    stats_ref[...] = jnp.where(lane == 0, mean, jnp.where(lane == 1, inv, gate))
    half_gate = 0.5 * gate
    for i, up in enumerate((up_own, up_sib)):
        value = jnp.dot(normed, up[...], preferred_element_type=F32)
        s = jax.nn.sigmoid(value)
        cols = slice(i * hidden_dev, (i + 1) * hidden_dev)
        hidden_ref[:, cols] = (value * s).astype(BF16)
        slope_ref[:, cols] = half_gate * s * (1.0 + value * (1.0 - s))
    total = jnp.dot(hidden_ref[:, :hidden_dev], down_own[...], preferred_element_type=F32)
    total = total + jnp.dot(hidden_ref[:, hidden_dev:], down_sib[...], preferred_element_type=F32)
    total_ref[...] = (total * half_gate).astype(BF16)
    dissect(total_ref, outs, ways, width)


def forward(blocks, ways, weights, gain, router):
    half, width = blocks[0].shape
    features, hidden_dev = weights[0].shape
    piece = jax.ShapeDtypeStruct((half, width), BF16)
    got = call(
        functools.partial(forward_body, ways, width),
        "forward",
        (piece,) * len(ways)
        + (
            jax.ShapeDtypeStruct((half, features), BF16),
            jax.ShapeDtypeStruct((half, 128), F32),
            jax.ShapeDtypeStruct((half, 2 * hidden_dev), BF16),
            jax.ShapeDtypeStruct((half, 2 * hidden_dev), F32),
        ),
        (*blocks, *weights, gain, router),
        [vspec()] * (len(blocks) + 6),
        [VMEM((half, features), BF16)],
        1,
        1,
        16,
    )
    return got[: len(ways)], got[len(ways) :]


def backward_body(ways, width, *refs):
    n = len(ways)
    blocks = refs[:n]
    up_own, up_sib, down_own, down_sib, gain_ref, router_ref = refs[n : n + 6]
    full_ref, stats_ref, hidden_ref, slope_ref = refs[n + 6 : n + 10]
    outs = refs[n + 10 : 2 * n + 10]
    (cot_ref,) = refs[2 * n + 10 :]
    assemble(cot_ref, blocks, ways, width)
    half, features = full_ref.shape
    hidden_dev = up_own.shape[1]
    score, pre = 0.0, []
    for i, down in enumerate((down_own, down_sib)):
        value = lax.dot_general(cot_ref[...], down[...], OVER_LANES, preferred_element_type=F32)
        cols = slice(i * hidden_dev, (i + 1) * hidden_dev)
        pre.append((value * slope_ref[:, cols]).astype(BF16))
        score = score + jnp.sum(value * hidden_ref[:, cols].astype(F32), axis=1, keepdims=True)
    scaled = lax.dot_general(pre[0], up_own[...], OVER_LANES, preferred_element_type=F32)
    scaled = scaled + lax.dot_general(pre[1], up_sib[...], OVER_LANES, preferred_element_type=F32)
    scaled = scaled * gain_ref[...].reshape(1, features)
    mean, inv, gate = stats_ref[:, 0:1], stats_ref[:, 1:2], stats_ref[:, 2:3]
    centred = (full_ref[...].astype(F32) - mean) * inv
    plain = jnp.sum(scaled, axis=1, keepdims=True) * (1.0 / features)
    cross = jnp.sum(scaled * centred, axis=1, keepdims=True) * (1.0 / features)
    term = 0.5 * score * gate * (1.0 - gate)
    cot_ref[...] = (inv * (scaled - plain - centred * cross) + term * router_ref[...].reshape(1, features)).astype(BF16)
    dissect(cot_ref, outs, ways, width)


def backward(blocks, ways, weights, gain, router, saved):
    half, width = blocks[0].shape
    features, hidden_dev = weights[0].shape
    return call(
        functools.partial(backward_body, ways, width),
        "backward",
        (jax.ShapeDtypeStruct((half, width), BF16),) * len(ways),
        (*blocks, *weights, gain, router, *saved),
        [vspec()] * (len(blocks) + 10),
        [VMEM((half, features), BF16)],
        1,
        1,
        16,
    )


def after(value, *others):
    return lax.optimization_barrier((value, *others))[0]


def per_device(frames, router_weight, norm_gain, up_weight, down_weight, picked_rows, picked_count, cotangent):
    width = frames.shape[1]
    features = up_weight.shape[0]
    half = picked_rows.shape[0] // 2
    tensors = lax.axis_size("tensor")
    gain, router = norm_gain, router_weight
    steps = range(1, tensors)
    aligned = width % 128 == 0
    pieces = [(0, 0), (0, 1)] + [(k, 0) for k in steps] + [(k, 1) for k in steps]
    ways = pieces if aligned else [(0, 0)]

    def send(x, k, side):
        pairs = [
            (chip * 2 + core, (chip + k) % tensors * 2 + (core + side) % 2) for chip in range(tensors) for core in (0, 1)
        ]
        return lax.ppermute(x, ("tensor", "pair"), pairs)

    def swap(x):
        return lax.ppermute(x, "pair", [(0, 1), (1, 0)])

    def joined(blocks):
        if aligned:
            return blocks
        full = jnp.zeros((half, features), BF16)
        for (k, side), block in zip(pieces, blocks):
            full = lax.dynamic_update_slice_in_dim(full, block, block_start(-k, side, width), 1)
        return [full]

    def cut(outs):
        if aligned:
            return outs
        return [lax.dynamic_slice_in_dim(outs[0], block_start(k, side, width), width, 1) for k, side in pieces]

    def collect(mine, sib):
        return [mine, swap(sib)] + [send(mine, k, 0) for k in steps] + [send(sib, k, 1) for k in steps]

    def deliver(parts):
        count = tensors - 1
        far_mine = [send(x, k, 0) for x, k in zip(parts[2 : 2 + count], steps)]
        far_sib = [send(x, k, 1) for x, k in zip(parts[2 + count :], steps)]
        return [parts[0]] + far_mine, [swap(parts[1])] + far_sib

    up_sib, down_sib = swap(up_weight), swap(down_weight)
    weights = (up_weight, up_sib, down_weight, down_sib)
    mine, sib, wanted = gather_rows(picked_count, picked_rows, frames, 1)
    blocks = collect(mine, sib)
    cot_mine, cot_sib, _ = gather_rows(picked_count, picked_rows, cotangent, 1)
    cot_mine, cot_sib = lax.optimization_barrier((cot_mine, cot_sib, blocks[1], up_sib, down_sib))[:2]
    cot_blocks = collect(cot_mine, cot_sib)
    parts, saved = forward(joined(blocks), ways, weights, gain, router)
    out_mine, out_sib = deliver(cut(parts))
    grads = backward(joined(cot_blocks), ways, weights, gain, router, saved)
    grad_mine, grad_sib = deliver(cut(grads))
    mixed = scatter_rows("mixed_rows", wanted, frames, out_mine, out_sib)
    grad_mine[0] = after(grad_mine[0], mixed)
    frames_grad = scatter_rows("grad_rows", wanted, cotangent, grad_mine, grad_sib)
    return (mixed, frames_grad)


def solution(mesh):
    return jax.shard_map(
        per_device,
        mesh=mesh,
        in_specs=(
            P(("group", "tm"), ("tensor", "pair")),
            P(),
            P(),
            P(None, ("tensor", "pair")),
            P(("tensor", "pair"), None),
            P(("group", "tm")),
            P("group"),
            P(("group", "tm"), ("tensor", "pair")),
        ),
        out_specs=(P(("group", "tm"), ("tensor", "pair")), P(("group", "tm"), ("tensor", "pair"))),
        check_vma=False,
    )
```

```python
import functools

import jax
import jax.numpy as jnp
from jax import lax
from jax.experimental import pallas as pl
from jax.experimental.pallas import tpu as pltpu
from jax.sharding import PartitionSpec as P

EPS = 1e-05
F32 = jnp.float32
BF16 = jnp.bfloat16
VMEM = pltpu.VMEM
ANY = pl.BlockSpec(memory_space=pl.ANY)
OVER_LANES = (((1,), (1,)), ((), ()))


def vspec():
    return pl.BlockSpec(memory_space=VMEM)


def call(body, name, outs, ins, specs, scratch, flops, moved, limit):
    return pl.pallas_call(
        body,
        out_shape=outs,
        in_specs=specs,
        out_specs=jax.tree.map(lambda _: vspec(), outs),
        scratch_shapes=scratch,
        compiler_params=pltpu.CompilerParams(vmem_limit_bytes=limit * 1024 * 1024),
        cost_estimate=pl.CostEstimate(flops=flops, bytes_accessed=moved, transcendentals=0),
        name=name,
    )(*ins)


def chunks_of(extent):
    size = 512 if extent % 512 == 0 else extent
    return [(start, size) for start in range(0, extent, size)]


def fetch(sources, targets, sems):
    copies = [pltpu.make_async_copy(s, t, sems.at[i]) for i, (s, t) in enumerate(zip(sources, targets))]
    for copy in copies:
        copy.start()
    return copies


def call_in_hbm(body, name, outs, ins, scratch, flops, moved):
    return pl.pallas_call(
        body,
        out_shape=outs,
        in_specs=[ANY] * len(ins),
        out_specs=jax.tree.map(lambda _: ANY, outs),
        scratch_shapes=scratch,
        compiler_params=pltpu.CompilerParams(vmem_limit_bytes=56 * 1024 * 1024),
        cost_estimate=pl.CostEstimate(flops=flops, bytes_accessed=moved, transcendentals=0),
        name=name,
    )(*ins)


def wanted_slots(count, picked):
    slots = picked.shape[0]
    live = lax.broadcasted_iota(jnp.int32, (8, slots), 1) < count
    wanted = jnp.where(live, jnp.broadcast_to(picked.reshape(1, slots), (8, slots)), -1)
    swapped = pltpu.roll(wanted, slots // 2, 1)
    return jnp.where(lax.axis_index("pair") == 0, wanted, swapped)[:1]


def gather_body(count_hbm, picked_hbm, frames_hbm, mine_hbm, sib_hbm, wanted_hbm, frames, picked, count, mine, sib, sems):
    slots = picked.shape[0]
    frames_dev = frames.shape[0]
    copies = fetch((frames_hbm, picked_hbm, count_hbm), (frames, picked, count), sems)
    copies[1].wait()
    copies[2].wait()
    wanted = wanted_slots(count[lax.axis_index("tm")], picked[...])
    picked[...] = wanted.reshape(slots)
    column = jnp.broadcast_to(wanted.astype(F32), (128, slots)).T[:, :1]
    place = lax.broadcasted_iota(jnp.int32, (1, frames_dev), 1).astype(F32)
    onehot = jnp.where(column == place, 1.0, 0.0).astype(BF16)
    copies[0].wait()
    rows = jnp.dot(onehot, frames[...], preferred_element_type=F32).astype(BF16)
    half = mine.shape[0]
    mine[...] = rows[:half]
    sib[...] = rows[half:]
    for copy in fetch((sib, mine, picked), (sib_hbm, mine_hbm, wanted_hbm), sems):
        copy.wait()


def gather_rows(count, picked, frames, moved):
    slots, (frames_dev, width) = picked.shape[0], frames.shape
    out = jax.ShapeDtypeStruct((slots // 2, width), BF16)
    return call_in_hbm(
        gather_body,
        "gather_rows",
        (out, out, jax.ShapeDtypeStruct(picked.shape, jnp.int32)),
        (count, picked, frames),
        [
            VMEM(frames.shape, BF16),
            VMEM(picked.shape, jnp.int32),
            pltpu.SMEM(count.shape, jnp.int32),
            VMEM(out.shape, BF16),
            VMEM(out.shape, BF16),
            pltpu.SemaphoreType.DMA((3,)),
        ],
        2 * slots * frames_dev * width,
        moved,
    )


def scatter_body(mines, sibs, wanted_ref, frames_ref, *refs):
    parts, (out_hbm, out_ref, sems) = refs[: mines + sibs], refs[mines + sibs :]
    wanted = wanted_ref[...].reshape(1, wanted_ref.shape[0])

    def added(blocks):
        total = blocks[0][...].astype(F32)
        for block in blocks[1:]:
            total = total + block[...].astype(F32)
        return total.astype(BF16)

    rows = jnp.concatenate([added(parts[:mines]), added(parts[mines:])], axis=0)
    stores = []
    for i, (start, size) in enumerate(chunks_of(frames_ref.shape[0])):
        place = lax.broadcasted_iota(jnp.int32, (size, 1), 0) + start
        onehot = jnp.where(wanted == place, 1.0, 0.0).astype(BF16)
        put = jnp.dot(onehot, rows, preferred_element_type=F32)
        out_ref[start : start + size, :] = (frames_ref[start : start + size, :].astype(F32) + put).astype(BF16)
        cut = pl.ds(start, size)
        store = pltpu.make_async_copy(out_ref.at[cut], out_hbm.at[cut], sems.at[i])
        store.start()
        stores.append(store)
    for store in stores:
        store.wait()


def scatter_rows(name, wanted, frames, mine_parts, sib_parts):
    slots, (frames_dev, width) = wanted.shape[0], frames.shape
    parts = list(mine_parts) + list(sib_parts)
    return pl.pallas_call(
        functools.partial(scatter_body, len(mine_parts), len(sib_parts)),
        out_shape=jax.ShapeDtypeStruct(frames.shape, BF16),
        in_specs=[vspec(), vspec()] + [vspec()] * len(parts),
        out_specs=ANY,
        scratch_shapes=[VMEM(frames.shape, BF16), pltpu.SemaphoreType.DMA((len(chunks_of(frames_dev)),))],
        compiler_params=pltpu.CompilerParams(vmem_limit_bytes=8 * 1024 * 1024),
        cost_estimate=pl.CostEstimate(
            flops=2 * slots * frames_dev * width, bytes_accessed=4 * frames_dev * width, transcendentals=0
        ),
        name=name,
    )(wanted, frames, *parts)


def block_start(step, side, width):
    tensors = lax.axis_size("tensor")
    chip = (lax.axis_index("tensor") + tensors + step) % tensors
    return (chip * 2 + (lax.axis_index("pair") + side) % 2) * width


def assemble(full_ref, blocks, ways, width):
    if len(ways) == 1:
        full_ref[...] = blocks[0][...]
        return
    for (step, side), block in zip(ways, blocks):
        start = pl.multiple_of(block_start(-step, side, width), 128)
        full_ref[:, pl.ds(start, width)] = block[...]


def dissect(total_ref, outs, ways, width):
    if len(ways) == 1:
        outs[0][...] = total_ref[...]
        return
    for (step, side), out in zip(ways, outs):
        start = pl.multiple_of(block_start(step, side, width), 128)
        out[...] = total_ref[:, pl.ds(start, width)]


def forward_body(ways, width, *refs):
    n = len(ways)
    blocks = refs[:n]
    up_own, up_sib, down_own, down_sib, gain_ref, router_ref = refs[n : n + 6]
    outs = refs[n + 6 : 2 * n + 6]
    full_ref, stats_ref, hidden_ref, slope_ref = refs[2 * n + 6 : 2 * n + 10]
    (total_ref,) = refs[2 * n + 10 :]
    assemble(full_ref, blocks, ways, width)
    half, features = full_ref.shape
    hidden_dev = up_own.shape[1]
    wide = full_ref[...].astype(F32)
    gate = jax.nn.sigmoid(jnp.sum(wide * router_ref[...].reshape(1, features), axis=1, keepdims=True))
    mean = jnp.sum(wide, axis=1, keepdims=True) * (1.0 / features)
    deviate = wide - mean
    inv = lax.rsqrt(jnp.sum(deviate * deviate, axis=1, keepdims=True) * (1.0 / features) + EPS)
    normed = (deviate * inv * gain_ref[...].reshape(1, features)).astype(BF16)
    lane = lax.broadcasted_iota(jnp.int32, (half, 128), 1)
    stats_ref[...] = jnp.where(lane == 0, mean, jnp.where(lane == 1, inv, gate))
    half_gate = 0.5 * gate
    for i, up in enumerate((up_own, up_sib)):
        value = jnp.dot(normed, up[...], preferred_element_type=F32)
        s = jax.nn.sigmoid(value)
        cols = slice(i * hidden_dev, (i + 1) * hidden_dev)
        hidden_ref[:, cols] = (value * s).astype(BF16)
        slope_ref[:, cols] = half_gate * s * (1.0 + value * (1.0 - s))
    total = jnp.dot(hidden_ref[:, :hidden_dev], down_own[...], preferred_element_type=F32)
    total = total + jnp.dot(hidden_ref[:, hidden_dev:], down_sib[...], preferred_element_type=F32)
    total_ref[...] = (total * half_gate).astype(BF16)
    dissect(total_ref, outs, ways, width)


def forward(blocks, ways, weights, gain, router):
    half, width = blocks[0].shape
    features, hidden_dev = weights[0].shape
    piece = jax.ShapeDtypeStruct((half, width), BF16)
    got = call(
        functools.partial(forward_body, ways, width),
        "forward",
        (piece,) * len(ways)
        + (
            jax.ShapeDtypeStruct((half, features), BF16),
            jax.ShapeDtypeStruct((half, 128), F32),
            jax.ShapeDtypeStruct((half, 2 * hidden_dev), BF16),
            jax.ShapeDtypeStruct((half, 2 * hidden_dev), F32),
        ),
        (*blocks, *weights, gain, router),
        [vspec()] * (len(blocks) + 6),
        [VMEM((half, features), BF16)],
        1,
        1,
        16,
    )
    return got[: len(ways)], got[len(ways) :]


def backward_body(ways, width, *refs):
    n = len(ways)
    blocks = refs[:n]
    up_own, up_sib, down_own, down_sib, gain_ref, router_ref = refs[n : n + 6]
    full_ref, stats_ref, hidden_ref, slope_ref = refs[n + 6 : n + 10]
    outs = refs[n + 10 : 2 * n + 10]
    (cot_ref,) = refs[2 * n + 10 :]
    assemble(cot_ref, blocks, ways, width)
    half, features = full_ref.shape
    hidden_dev = up_own.shape[1]
    score, pre = 0.0, []
    for i, down in enumerate((down_own, down_sib)):
        value = lax.dot_general(cot_ref[...], down[...], OVER_LANES, preferred_element_type=F32)
        cols = slice(i * hidden_dev, (i + 1) * hidden_dev)
        pre.append((value * slope_ref[:, cols]).astype(BF16))
        score = score + jnp.sum(value * hidden_ref[:, cols].astype(F32), axis=1, keepdims=True)
    scaled = lax.dot_general(pre[0], up_own[...], OVER_LANES, preferred_element_type=F32)
    scaled = scaled + lax.dot_general(pre[1], up_sib[...], OVER_LANES, preferred_element_type=F32)
    scaled = scaled * gain_ref[...].reshape(1, features)
    mean, inv, gate = stats_ref[:, 0:1], stats_ref[:, 1:2], stats_ref[:, 2:3]
    centred = (full_ref[...].astype(F32) - mean) * inv
    plain = jnp.sum(scaled, axis=1, keepdims=True) * (1.0 / features)
    cross = jnp.sum(scaled * centred, axis=1, keepdims=True) * (1.0 / features)
    term = 0.5 * score * gate * (1.0 - gate)
    cot_ref[...] = (inv * (scaled - plain - centred * cross) + term * router_ref[...].reshape(1, features)).astype(BF16)
    dissect(cot_ref, outs, ways, width)


def backward(blocks, ways, weights, gain, router, saved):
    half, width = blocks[0].shape
    features, hidden_dev = weights[0].shape
    return call(
        functools.partial(backward_body, ways, width),
        "backward",
        (jax.ShapeDtypeStruct((half, width), BF16),) * len(ways),
        (*blocks, *weights, gain, router, *saved),
        [vspec()] * (len(blocks) + 10),
        [VMEM((half, features), BF16)],
        1,
        1,
        16,
    )


def after(value, *others):
    return lax.optimization_barrier((value, *others))[0]


def per_device(frames, router_weight, norm_gain, up_weight, down_weight, picked_rows, picked_count, cotangent):
    width = frames.shape[1]
    features = up_weight.shape[0]
    half = picked_rows.shape[0] // 2
    tensors = lax.axis_size("tensor")
    gain, router = norm_gain, router_weight
    steps = range(1, tensors)
    aligned = width % 128 == 0
    pieces = [(0, 0), (0, 1)] + [(k, 0) for k in steps] + [(k, 1) for k in steps]
    ways = pieces if aligned else [(0, 0)]

    def send(x, k, side):
        pairs = [
            (chip * 2 + core, (chip + k) % tensors * 2 + (core + side) % 2) for chip in range(tensors) for core in (0, 1)
        ]
        return lax.ppermute(x, ("tensor", "pair"), pairs)

    def swap(x):
        return lax.ppermute(x, "pair", [(0, 1), (1, 0)])

    def joined(blocks):
        if aligned:
            return blocks
        full = jnp.zeros((half, features), BF16)
        for (k, side), block in zip(pieces, blocks):
            full = lax.dynamic_update_slice_in_dim(full, block, block_start(-k, side, width), 1)
        return [full]

    def cut(outs):
        if aligned:
            return outs
        return [lax.dynamic_slice_in_dim(outs[0], block_start(k, side, width), width, 1) for k, side in pieces]

    def collect(mine, sib):
        return [mine, swap(sib)] + [send(mine, k, 0) for k in steps] + [send(sib, k, 1) for k in steps]

    def deliver(parts):
        count = tensors - 1
        far_mine = [send(x, k, 0) for x, k in zip(parts[2 : 2 + count], steps)]
        far_sib = [send(x, k, 1) for x, k in zip(parts[2 + count :], steps)]
        return [parts[0]] + far_mine, [swap(parts[1])] + far_sib

    mine, sib, wanted = gather_rows(picked_count, picked_rows, frames, 1)
    blocks = collect(mine, sib)
    up_sib, down_sib = swap(after(up_weight, mine)), swap(after(down_weight, mine))
    weights = (up_weight, up_sib, down_weight, down_sib)
    cot_mine, cot_sib, _ = gather_rows(picked_count, picked_rows, cotangent, 1)
    cot_mine, cot_sib = lax.optimization_barrier((cot_mine, cot_sib, up_sib))[:2]
    cot_blocks = collect(cot_mine, cot_sib)
    parts, saved = forward(joined(blocks), ways, weights, gain, router)
    out_mine, out_sib = deliver(cut(parts))
    grads = backward(joined(cot_blocks), ways, weights, gain, router, saved)
    grad_mine, grad_sib = deliver(cut(grads))
    mixed = scatter_rows("mixed_rows", wanted, frames, out_mine, out_sib)
    grad_mine[0] = after(grad_mine[0], mixed)
    frames_grad = scatter_rows("grad_rows", wanted, cotangent, grad_mine, grad_sib)
    return (mixed, frames_grad)


def solution(mesh):
    return jax.shard_map(
        per_device,
        mesh=mesh,
        in_specs=(
            P(("group", "tm"), ("tensor", "pair")),
            P(),
            P(),
            P(None, ("tensor", "pair")),
            P(("tensor", "pair"), None),
            P(("group", "tm")),
            P("group"),
            P(("group", "tm"), ("tensor", "pair")),
        ),
        out_specs=(P(("group", "tm"), ("tensor", "pair")), P(("group", "tm"), ("tensor", "pair"))),
        check_vma=False,
    )
```

```python
import functools

import jax
import jax.numpy as jnp
from jax import lax
from jax.experimental import pallas as pl
from jax.experimental.pallas import tpu as pltpu
from jax.sharding import PartitionSpec as P

EPS = 1e-05
F32 = jnp.float32
BF16 = jnp.bfloat16
VMEM = pltpu.VMEM
ANY = pl.BlockSpec(memory_space=pl.ANY)
OVER_LANES = (((1,), (1,)), ((), ()))


def vspec():
    return pl.BlockSpec(memory_space=VMEM)


def call(body, name, outs, ins, specs, scratch, flops, moved, limit):
    return pl.pallas_call(
        body,
        out_shape=outs,
        in_specs=specs,
        out_specs=jax.tree.map(lambda _: vspec(), outs),
        scratch_shapes=scratch,
        compiler_params=pltpu.CompilerParams(vmem_limit_bytes=limit * 1024 * 1024),
        cost_estimate=pl.CostEstimate(flops=flops, bytes_accessed=moved, transcendentals=0),
        name=name,
    )(*ins)


def chunks_of(extent):
    size = 512 if extent % 512 == 0 else extent
    return [(start, size) for start in range(0, extent, size)]


def fetch(sources, targets, sems):
    copies = [pltpu.make_async_copy(s, t, sems.at[i]) for i, (s, t) in enumerate(zip(sources, targets))]
    for copy in copies:
        copy.start()
    return copies


def call_in_hbm(body, name, outs, ins, scratch, flops, moved):
    return pl.pallas_call(
        body,
        out_shape=outs,
        in_specs=[ANY] * len(ins),
        out_specs=jax.tree.map(lambda _: ANY, outs),
        scratch_shapes=scratch,
        compiler_params=pltpu.CompilerParams(vmem_limit_bytes=56 * 1024 * 1024),
        cost_estimate=pl.CostEstimate(flops=flops, bytes_accessed=moved, transcendentals=0),
        name=name,
    )(*ins)


def wanted_slots(count, picked):
    slots = picked.shape[0]
    live = lax.broadcasted_iota(jnp.int32, (8, slots), 1) < count
    wanted = jnp.where(live, jnp.broadcast_to(picked.reshape(1, slots), (8, slots)), -1)
    swapped = pltpu.roll(wanted, slots // 2, 1)
    return jnp.where(lax.axis_index("pair") == 0, wanted, swapped)[:1]


def slots_body(count_hbm, picked_hbm, wanted_hbm, count, picked, sems):
    for copy in fetch((count_hbm, picked_hbm), (count, picked), sems):
        copy.wait()
    picked[...] = wanted_slots(count[lax.axis_index("tm")], picked[...]).reshape(picked.shape)
    for copy in fetch((picked,), (wanted_hbm,), sems):
        copy.wait()


def live_slots(count, picked):
    return call_in_hbm(
        slots_body,
        "live_slots",
        jax.ShapeDtypeStruct(picked.shape, jnp.int32),
        (count, picked),
        [pltpu.SMEM(count.shape, jnp.int32), VMEM(picked.shape, jnp.int32), pltpu.SemaphoreType.DMA((2,))],
        1,
        1,
    )


def gather_rows(places, frames):
    onehot = (lax.broadcasted_iota(jnp.int32, (frames.shape[0], 1), 0) == places).astype(BF16)
    return lax.dot_general(onehot, frames, (((0,), (0,)), ((), ())), preferred_element_type=F32).astype(BF16)


def scatter_body(mines, sibs, wanted_ref, frames_ref, *refs):
    parts, (out_hbm, out_ref, sems) = refs[: mines + sibs], refs[mines + sibs :]
    wanted = wanted_ref[...].reshape(1, wanted_ref.shape[0])

    def added(blocks):
        total = blocks[0][...].astype(F32)
        for block in blocks[1:]:
            total = total + block[...].astype(F32)
        return total.astype(BF16)

    rows = jnp.concatenate([added(parts[:mines]), added(parts[mines:])], axis=0)
    stores = []
    for i, (start, size) in enumerate(chunks_of(frames_ref.shape[0])):
        place = lax.broadcasted_iota(jnp.int32, (size, 1), 0) + start
        onehot = jnp.where(wanted == place, 1.0, 0.0).astype(BF16)
        put = jnp.dot(onehot, rows, preferred_element_type=F32)
        out_ref[start : start + size, :] = (frames_ref[start : start + size, :].astype(F32) + put).astype(BF16)
        cut = pl.ds(start, size)
        store = pltpu.make_async_copy(out_ref.at[cut], out_hbm.at[cut], sems.at[i])
        store.start()
        stores.append(store)
    for store in stores:
        store.wait()


def scatter_rows(name, wanted, frames, mine_parts, sib_parts):
    slots, (frames_dev, width) = wanted.shape[0], frames.shape
    parts = list(mine_parts) + list(sib_parts)
    return pl.pallas_call(
        functools.partial(scatter_body, len(mine_parts), len(sib_parts)),
        out_shape=jax.ShapeDtypeStruct(frames.shape, BF16),
        in_specs=[vspec(), vspec()] + [vspec()] * len(parts),
        out_specs=ANY,
        scratch_shapes=[VMEM(frames.shape, BF16), pltpu.SemaphoreType.DMA((len(chunks_of(frames_dev)),))],
        compiler_params=pltpu.CompilerParams(vmem_limit_bytes=8 * 1024 * 1024),
        cost_estimate=pl.CostEstimate(
            flops=2 * slots * frames_dev * width, bytes_accessed=4 * frames_dev * width, transcendentals=0
        ),
        name=name,
    )(wanted, frames, *parts)


def block_start(step, side, width):
    tensors = lax.axis_size("tensor")
    chip = (lax.axis_index("tensor") + tensors + step) % tensors
    return (chip * 2 + (lax.axis_index("pair") + side) % 2) * width


def assemble(full_ref, blocks, ways, width):
    if len(ways) == 1:
        full_ref[...] = blocks[0][...]
        return
    for (step, side), block in zip(ways, blocks):
        start = pl.multiple_of(block_start(-step, side, width), 128)
        full_ref[:, pl.ds(start, width)] = block[...]


def dissect(total_ref, outs, ways, width):
    if len(ways) == 1:
        outs[0][...] = total_ref[...]
        return
    for (step, side), out in zip(ways, outs):
        start = pl.multiple_of(block_start(step, side, width), 128)
        out[...] = total_ref[:, pl.ds(start, width)]


def forward_body(ways, width, *refs):
    n = len(ways)
    blocks = refs[:n]
    up_own, up_sib, down_own, down_sib, gain_ref, router_ref = refs[n : n + 6]
    outs = refs[n + 6 : 2 * n + 6]
    full_ref, stats_ref, hidden_ref, slope_ref = refs[2 * n + 6 : 2 * n + 10]
    (total_ref,) = refs[2 * n + 10 :]
    assemble(full_ref, blocks, ways, width)
    half, features = full_ref.shape
    hidden_dev = up_own.shape[1]
    wide = full_ref[...].astype(F32)
    gate = jax.nn.sigmoid(jnp.sum(wide * router_ref[...].reshape(1, features), axis=1, keepdims=True))
    mean = jnp.sum(wide, axis=1, keepdims=True) * (1.0 / features)
    deviate = wide - mean
    inv = lax.rsqrt(jnp.sum(deviate * deviate, axis=1, keepdims=True) * (1.0 / features) + EPS)
    normed = (deviate * inv * gain_ref[...].reshape(1, features)).astype(BF16)
    lane = lax.broadcasted_iota(jnp.int32, (half, 128), 1)
    stats_ref[...] = jnp.where(lane == 0, mean, jnp.where(lane == 1, inv, gate))
    half_gate = 0.5 * gate
    for i, up in enumerate((up_own, up_sib)):
        value = jnp.dot(normed, up[...], preferred_element_type=F32)
        s = jax.nn.sigmoid(value)
        cols = slice(i * hidden_dev, (i + 1) * hidden_dev)
        hidden_ref[:, cols] = (value * s).astype(BF16)
        slope_ref[:, cols] = half_gate * s * (1.0 + value * (1.0 - s))
    total = jnp.dot(hidden_ref[:, :hidden_dev], down_own[...], preferred_element_type=F32)
    total = total + jnp.dot(hidden_ref[:, hidden_dev:], down_sib[...], preferred_element_type=F32)
    total_ref[...] = (total * half_gate).astype(BF16)
    dissect(total_ref, outs, ways, width)


def forward(blocks, ways, weights, gain, router):
    half, width = blocks[0].shape
    features, hidden_dev = weights[0].shape
    piece = jax.ShapeDtypeStruct((half, width), BF16)
    got = call(
        functools.partial(forward_body, ways, width),
        "forward",
        (piece,) * len(ways)
        + (
            jax.ShapeDtypeStruct((half, features), BF16),
            jax.ShapeDtypeStruct((half, 128), F32),
            jax.ShapeDtypeStruct((half, 2 * hidden_dev), BF16),
            jax.ShapeDtypeStruct((half, 2 * hidden_dev), F32),
        ),
        (*blocks, *weights, gain, router),
        [vspec()] * (len(blocks) + 6),
        [VMEM((half, features), BF16)],
        1,
        1,
        16,
    )
    return got[: len(ways)], got[len(ways) :]


def backward_body(ways, width, *refs):
    n = len(ways)
    blocks = refs[:n]
    up_own, up_sib, down_own, down_sib, gain_ref, router_ref = refs[n : n + 6]
    full_ref, stats_ref, hidden_ref, slope_ref = refs[n + 6 : n + 10]
    outs = refs[n + 10 : 2 * n + 10]
    (cot_ref,) = refs[2 * n + 10 :]
    assemble(cot_ref, blocks, ways, width)
    half, features = full_ref.shape
    hidden_dev = up_own.shape[1]
    score, pre = 0.0, []
    for i, down in enumerate((down_own, down_sib)):
        value = lax.dot_general(cot_ref[...], down[...], OVER_LANES, preferred_element_type=F32)
        cols = slice(i * hidden_dev, (i + 1) * hidden_dev)
        pre.append((value * slope_ref[:, cols]).astype(BF16))
        score = score + jnp.sum(value * hidden_ref[:, cols].astype(F32), axis=1, keepdims=True)
    scaled = lax.dot_general(pre[0], up_own[...], OVER_LANES, preferred_element_type=F32)
    scaled = scaled + lax.dot_general(pre[1], up_sib[...], OVER_LANES, preferred_element_type=F32)
    scaled = scaled * gain_ref[...].reshape(1, features)
    mean, inv, gate = stats_ref[:, 0:1], stats_ref[:, 1:2], stats_ref[:, 2:3]
    centred = (full_ref[...].astype(F32) - mean) * inv
    plain = jnp.sum(scaled, axis=1, keepdims=True) * (1.0 / features)
    cross = jnp.sum(scaled * centred, axis=1, keepdims=True) * (1.0 / features)
    term = 0.5 * score * gate * (1.0 - gate)
    cot_ref[...] = (inv * (scaled - plain - centred * cross) + term * router_ref[...].reshape(1, features)).astype(BF16)
    dissect(cot_ref, outs, ways, width)


def backward(blocks, ways, weights, gain, router, saved):
    half, width = blocks[0].shape
    features, hidden_dev = weights[0].shape
    return call(
        functools.partial(backward_body, ways, width),
        "backward",
        (jax.ShapeDtypeStruct((half, width), BF16),) * len(ways),
        (*blocks, *weights, gain, router, *saved),
        [vspec()] * (len(blocks) + 10),
        [VMEM((half, features), BF16)],
        1,
        1,
        16,
    )


def after(value, *others):
    return lax.optimization_barrier((value, *others))[0]


def per_device(frames, router_weight, norm_gain, up_weight, down_weight, picked_rows, picked_count, cotangent):
    width = frames.shape[1]
    features = up_weight.shape[0]
    half = picked_rows.shape[0] // 2
    tensors = lax.axis_size("tensor")
    gain, router = norm_gain, router_weight
    steps = range(1, tensors)
    aligned = width % 128 == 0
    pieces = [(0, 0), (0, 1)] + [(k, 0) for k in steps] + [(k, 1) for k in steps]
    ways = pieces if aligned else [(0, 0)]

    def send(x, k, side):
        pairs = [
            (chip * 2 + core, (chip + k) % tensors * 2 + (core + side) % 2) for chip in range(tensors) for core in (0, 1)
        ]
        return lax.ppermute(x, ("tensor", "pair"), pairs)

    def swap(x):
        return lax.ppermute(x, "pair", [(0, 1), (1, 0)])

    def joined(blocks):
        if aligned:
            return blocks
        full = jnp.zeros((half, features), BF16)
        for (k, side), block in zip(pieces, blocks):
            full = lax.dynamic_update_slice_in_dim(full, block, block_start(-k, side, width), 1)
        return [full]

    def cut(outs):
        if aligned:
            return outs
        return [lax.dynamic_slice_in_dim(outs[0], block_start(k, side, width), width, 1) for k, side in pieces]

    def collect(mine, sib):
        return [mine, swap(sib)] + [send(mine, k, 0) for k in steps] + [send(sib, k, 1) for k in steps]

    def deliver(parts):
        count = tensors - 1
        far_mine = [send(x, k, 0) for x, k in zip(parts[2 : 2 + count], steps)]
        far_sib = [send(x, k, 1) for x, k in zip(parts[2 + count :], steps)]
        return [parts[0]] + far_mine, [swap(parts[1])] + far_sib

    wanted = live_slots(picked_count, picked_rows)
    first = lax.axis_index("pair") == 0
    places_mine = jnp.where(first, picked_rows[:half], picked_rows[half:])
    places_sib = jnp.where(first, picked_rows[half:], picked_rows[:half])
    mine, sib = gather_rows(places_mine, frames), gather_rows(places_sib, frames)
    blocks = collect(mine, sib)
    up_sib, down_sib = swap(after(up_weight, mine)), swap(after(down_weight, mine))
    weights = (up_weight, up_sib, down_weight, down_sib)
    rows = gather_rows(jnp.concatenate([places_mine, places_sib]), cotangent)
    cot_mine, cot_sib = lax.optimization_barrier((rows[:half], rows[half:]))
    cot_mine, cot_sib = lax.optimization_barrier((cot_mine, cot_sib, up_sib))[:2]
    cot_blocks = collect(cot_mine, cot_sib)
    parts, saved = forward(joined(blocks), ways, weights, gain, router)
    out_mine, out_sib = deliver(cut(parts))
    grads = backward(joined(cot_blocks), ways, weights, gain, router, saved)
    grad_mine, grad_sib = deliver(cut(grads))
    mixed = scatter_rows("mixed_rows", wanted, frames, out_mine, out_sib)
    grad_mine[0] = after(grad_mine[0], mixed)
    frames_grad = scatter_rows("grad_rows", wanted, cotangent, grad_mine, grad_sib)
    return (mixed, frames_grad)


def solution(mesh):
    return jax.shard_map(
        per_device,
        mesh=mesh,
        in_specs=(
            P(("group", "tm"), ("tensor", "pair")),
            P(),
            P(),
            P(None, ("tensor", "pair")),
            P(("tensor", "pair"), None),
            P(("group", "tm")),
            P("group"),
            P(("group", "tm"), ("tensor", "pair")),
        ),
        out_specs=(P(("group", "tm"), ("tensor", "pair")), P(("group", "tm"), ("tensor", "pair"))),
        check_vma=False,
    )
```

```python
import functools

import jax
import jax.numpy as jnp
from jax import lax
from jax.experimental import pallas as pl
from jax.experimental.pallas import tpu as pltpu
from jax.sharding import PartitionSpec as P

EPS = 1e-05
F32 = jnp.float32
BF16 = jnp.bfloat16
VMEM = pltpu.VMEM
ANY = pl.BlockSpec(memory_space=pl.ANY)
OVER_LANES = (((1,), (1,)), ((), ()))


def vspec():
    return pl.BlockSpec(memory_space=VMEM)


def call(body, name, outs, ins, specs, scratch, flops, moved, limit):
    return pl.pallas_call(
        body,
        out_shape=outs,
        in_specs=specs,
        out_specs=jax.tree.map(lambda _: vspec(), outs),
        scratch_shapes=scratch,
        compiler_params=pltpu.CompilerParams(vmem_limit_bytes=limit * 1024 * 1024),
        cost_estimate=pl.CostEstimate(flops=flops, bytes_accessed=moved, transcendentals=0),
        name=name,
    )(*ins)


def chunks_of(extent):
    size = 256 if extent % 256 == 0 else extent
    return [(start, size) for start in range(0, extent, size)]


def wanted_slots(count_ref, picked_ref):
    slots, indices = picked_ref.shape[0], count_ref.shape[0]
    here = lax.broadcasted_iota(jnp.int32, (1, indices), 1) == lax.axis_index("tm")
    count = jnp.sum(jnp.where(here, count_ref[...].reshape(1, indices), 0), axis=1, keepdims=True)
    live = lax.broadcasted_iota(jnp.int32, (8, slots), 1) < count
    wanted = jnp.where(live, jnp.broadcast_to(picked_ref[...].reshape(1, slots), (8, slots)), -1)
    swapped = pltpu.roll(wanted, slots // 2, 1)
    first = lax.axis_index("pair") == 0
    return [jnp.where(first, x, y)[:1, : slots // 2] for x, y in ((wanted, swapped), (swapped, wanted))]


def gather_rows(places, frames):
    onehot = (lax.broadcasted_iota(jnp.int32, (frames.shape[0], 1), 0) == places).astype(BF16)
    return lax.dot_general(onehot, frames, (((0,), (0,)), ((), ())), preferred_element_type=F32).astype(BF16)


def scatter_body(counts, frames_ref, *refs):
    groups, at = [], 0
    for n in counts:
        rows = refs[at + 1][...].astype(F32)
        for ref in refs[at + 2 : at + 1 + n]:
            rows = rows + ref[...].astype(F32)
        groups.append((refs[at][...].reshape(1, refs[at].shape[0]), rows.astype(BF16)))
        at += 1 + n
    out_ref, *scratch = refs[at:]
    stores = []
    for i, (start, size) in enumerate(chunks_of(frames_ref.shape[0])):
        place = lax.broadcasted_iota(jnp.int32, (size, 1), 0) + start
        total = frames_ref[start : start + size, :].astype(F32)
        for wanted, rows in groups:
            onehot = jnp.where(wanted == place, 1.0, 0.0).astype(BF16)
            total = total + jnp.dot(onehot, rows, preferred_element_type=F32)
        if not scratch:
            out_ref[start : start + size, :] = total.astype(BF16)
            continue
        staged, sems = scratch
        staged[start : start + size, :] = total.astype(BF16)
        cut = pl.ds(start, size)
        store = pltpu.make_async_copy(staged.at[cut], out_ref.at[cut], sems.at[i])
        store.start()
        stores.append(store)
    for store in stores:
        store.wait()


def scatter_rows(name, frames, groups, last=True):
    operands = [x for wanted, parts in groups for x in (wanted, *parts)]
    staging = [VMEM(frames.shape, BF16), pltpu.SemaphoreType.DMA((len(chunks_of(frames.shape[0])),))]
    return pl.pallas_call(
        functools.partial(scatter_body, [len(parts) for _, parts in groups]),
        out_shape=jax.ShapeDtypeStruct(frames.shape, BF16),
        in_specs=[vspec()] * (1 + len(operands)),
        out_specs=ANY if last else vspec(),
        scratch_shapes=staging if last else [],
        compiler_params=pltpu.CompilerParams(vmem_limit_bytes=8 * 1024 * 1024),
        name=name,
    )(frames, *operands)


def block_start(step, side, width):
    tensors = lax.axis_size("tensor")
    chip = (lax.axis_index("tensor") + tensors + step) % tensors
    return (chip * 2 + (lax.axis_index("pair") + side) % 2) * width


def assemble(full_ref, blocks, ways, width):
    if len(ways) == 1:
        full_ref[...] = blocks[0][...]
        return
    for (step, side), block in zip(ways, blocks):
        start = pl.multiple_of(block_start(-step, side, width), 128)
        full_ref[:, pl.ds(start, width)] = block[...]


def dissect(total_ref, outs, ways, width):
    if len(ways) == 1:
        outs[0][...] = total_ref[...]
        return
    for (step, side), out in zip(ways, outs):
        start = pl.multiple_of(block_start(step, side, width), 128)
        out[...] = total_ref[:, pl.ds(start, width)]


def forward_body(ways, width, count_ref, picked_ref, *refs):
    n = len(ways)
    blocks = refs[:n]
    up_own, up_sib, down_own, down_sib, gain_ref, router_ref = refs[n : n + 6]
    outs = refs[n + 6 : 2 * n + 6]
    full_ref, stats_ref, hidden_ref, slope_ref = refs[2 * n + 6 : 2 * n + 10]
    mine_ref, sib_ref, total_ref = refs[2 * n + 10 :]
    mine_ref[...], sib_ref[...] = [x.reshape(mine_ref.shape) for x in wanted_slots(count_ref, picked_ref)]
    assemble(full_ref, blocks, ways, width)
    half, features = full_ref.shape
    hidden_dev = up_own.shape[1]
    wide = full_ref[...].astype(F32)
    gate = jax.nn.sigmoid(jnp.sum(wide * router_ref[...].reshape(1, features), axis=1, keepdims=True))
    mean = jnp.sum(wide, axis=1, keepdims=True) * (1.0 / features)
    deviate = wide - mean
    inv = lax.rsqrt(jnp.sum(deviate * deviate, axis=1, keepdims=True) * (1.0 / features) + EPS)
    normed = (deviate * inv * gain_ref[...].reshape(1, features)).astype(BF16)
    lane = lax.broadcasted_iota(jnp.int32, (half, 128), 1)
    stats_ref[...] = jnp.where(lane == 0, mean, jnp.where(lane == 1, inv, gate))
    half_gate = 0.5 * gate
    for i, up in enumerate((up_own, up_sib)):
        value = jnp.dot(normed, up[...], preferred_element_type=F32)
        s = jax.nn.sigmoid(value)
        cols = slice(i * hidden_dev, (i + 1) * hidden_dev)
        hidden_ref[:, cols] = (value * s).astype(BF16)
        slope_ref[:, cols] = half_gate * s * (1.0 + value * (1.0 - s))
    total = jnp.dot(hidden_ref[:, :hidden_dev], down_own[...], preferred_element_type=F32)
    total = total + jnp.dot(hidden_ref[:, hidden_dev:], down_sib[...], preferred_element_type=F32)
    total_ref[...] = (total * half_gate).astype(BF16)
    dissect(total_ref, outs, ways, width)


def forward(count, picked, blocks, ways, weights, gain, router):
    half, width = blocks[0].shape
    features, hidden_dev = weights[0].shape
    piece = jax.ShapeDtypeStruct((half, width), BF16)
    got = call(
        functools.partial(forward_body, ways, width),
        "forward",
        (piece,) * len(ways)
        + (
            jax.ShapeDtypeStruct((half, features), BF16),
            jax.ShapeDtypeStruct((half, 128), F32),
            jax.ShapeDtypeStruct((half, 2 * hidden_dev), BF16),
            jax.ShapeDtypeStruct((half, 2 * hidden_dev), F32),
        )
        + (jax.ShapeDtypeStruct((half,), jnp.int32),) * 2,
        (count, picked, *blocks, *weights, gain, router),
        [vspec()] * (len(blocks) + 8),
        [VMEM((half, features), BF16)],
        1,
        1,
        16,
    )
    return got[: len(ways)], got[len(ways) : -2], got[-2:]


def backward_body(ways, width, *refs):
    n = len(ways)
    blocks = refs[:n]
    up_own, up_sib, down_own, down_sib, gain_ref, router_ref = refs[n : n + 6]
    full_ref, stats_ref, hidden_ref, slope_ref = refs[n + 6 : n + 10]
    outs = refs[n + 10 : 2 * n + 10]
    (cot_ref,) = refs[2 * n + 10 :]
    assemble(cot_ref, blocks, ways, width)
    half, features = full_ref.shape
    hidden_dev = up_own.shape[1]
    score, pre = 0.0, []
    for i, down in enumerate((down_own, down_sib)):
        value = lax.dot_general(cot_ref[...], down[...], OVER_LANES, preferred_element_type=F32)
        cols = slice(i * hidden_dev, (i + 1) * hidden_dev)
        pre.append((value * slope_ref[:, cols]).astype(BF16))
        score = score + jnp.sum(value * hidden_ref[:, cols].astype(F32), axis=1, keepdims=True)
    scaled = lax.dot_general(pre[0], up_own[...], OVER_LANES, preferred_element_type=F32)
    scaled = scaled + lax.dot_general(pre[1], up_sib[...], OVER_LANES, preferred_element_type=F32)
    scaled = scaled * gain_ref[...].reshape(1, features)
    mean, inv, gate = stats_ref[:, 0:1], stats_ref[:, 1:2], stats_ref[:, 2:3]
    centred = (full_ref[...].astype(F32) - mean) * inv
    plain = jnp.sum(scaled, axis=1, keepdims=True) * (1.0 / features)
    cross = jnp.sum(scaled * centred, axis=1, keepdims=True) * (1.0 / features)
    term = 0.5 * score * gate * (1.0 - gate)
    cot_ref[...] = (inv * (scaled - plain - centred * cross) + term * router_ref[...].reshape(1, features)).astype(BF16)
    dissect(cot_ref, outs, ways, width)


def backward(blocks, ways, weights, gain, router, saved):
    half, width = blocks[0].shape
    features, hidden_dev = weights[0].shape
    return call(
        functools.partial(backward_body, ways, width),
        "backward",
        (jax.ShapeDtypeStruct((half, width), BF16),) * len(ways),
        (*blocks, *weights, gain, router, *saved),
        [vspec()] * (len(blocks) + 10),
        [VMEM((half, features), BF16)],
        1,
        1,
        16,
    )


def after(value, *others):
    return lax.optimization_barrier((value, *others))[0]


def per_device(frames, router_weight, norm_gain, up_weight, down_weight, picked_rows, picked_count, cotangent):
    width = frames.shape[1]
    features = up_weight.shape[0]
    half = picked_rows.shape[0] // 2
    tensors = lax.axis_size("tensor")
    gain, router = norm_gain, router_weight
    steps = range(1, tensors)
    aligned = width % 128 == 0
    pieces = [(0, 0), (0, 1)] + [(k, 0) for k in steps] + [(k, 1) for k in steps]
    ways = pieces if aligned else [(0, 0)]

    def send(x, k, side):
        pairs = [
            (chip * 2 + core, (chip + k) % tensors * 2 + (core + side) % 2) for chip in range(tensors) for core in (0, 1)
        ]
        return lax.ppermute(x, ("tensor", "pair"), pairs)

    def swap(x):
        return lax.ppermute(x, "pair", [(0, 1), (1, 0)])

    def joined(blocks):
        if aligned:
            return blocks
        full = jnp.zeros((half, features), BF16)
        for (k, side), block in zip(pieces, blocks):
            full = lax.dynamic_update_slice_in_dim(full, block, block_start(-k, side, width), 1)
        return [full]

    def cut(outs):
        if aligned:
            return outs
        return [lax.dynamic_slice_in_dim(outs[0], block_start(k, side, width), width, 1) for k, side in pieces]

    def collect(mine, sib, near):
        return [mine, swap(near)] + [send(mine, k, 0) for k in steps] + [send(sib, k, 1) for k in steps]

    def deliver(parts):
        count = tensors - 1
        far_mine = [send(x, k, 0) for x, k in zip(parts[2 : 2 + count], steps)]
        far_sib = [send(x, k, 1) for x, k in zip(parts[2 + count :], steps)]
        return [parts[0]] + far_mine, [swap(parts[1])] + far_sib

    first = lax.axis_index("pair") == 0
    places_mine = jnp.where(first, picked_rows[:half], picked_rows[half:])
    places_sib = jnp.where(first, picked_rows[half:], picked_rows[:half])
    mine, sib = gather_rows(places_mine, frames), gather_rows(places_sib, frames)
    blocks = collect(mine, sib, after(sib, mine))
    up_sib, down_sib = swap(after(up_weight, mine)), swap(after(down_weight, mine))
    weights = (up_weight, up_sib, down_weight, down_sib)
    rows = gather_rows(jnp.concatenate([places_mine, places_sib]), cotangent)
    cot_mine, cot_sib = lax.optimization_barrier((rows[:half], rows[half:]))
    cot_mine, cot_sib = lax.optimization_barrier((cot_mine, cot_sib, up_sib))[:2]
    cot_blocks = collect(cot_mine, cot_sib, cot_sib)
    parts, saved, wanted = forward(picked_count, picked_rows, joined(blocks), ways, weights, gain, router)
    out_mine, out_sib = deliver(cut(parts))
    grads = backward(joined(cot_blocks), ways, weights, gain, router, saved)
    grad_mine, grad_sib = deliver(cut(grads))
    mixed = scatter_rows("mixed_rows", frames, [(wanted[0], out_mine), (wanted[1], out_sib)])
    grad_mine[0] = after(grad_mine[0], mixed)
    started = scatter_rows("grad_rows_mine", cotangent, [(wanted[0], grad_mine)], last=False)
    frames_grad = scatter_rows("grad_rows", started, [(wanted[1], grad_sib)])
    return (mixed, frames_grad)


def solution(mesh):
    return jax.shard_map(
        per_device,
        mesh=mesh,
        in_specs=(
            P(("group", "tm"), ("tensor", "pair")),
            P(),
            P(),
            P(None, ("tensor", "pair")),
            P(("tensor", "pair"), None),
            P(("group", "tm")),
            P("group"),
            P(("group", "tm"), ("tensor", "pair")),
        ),
        out_specs=(P(("group", "tm"), ("tensor", "pair")), P(("group", "tm"), ("tensor", "pair"))),
        check_vma=False,
    )
```

```python
import functools

import jax
import jax.numpy as jnp
from jax import lax
from jax.experimental import pallas as pl
from jax.experimental.pallas import tpu as pltpu
from jax.sharding import PartitionSpec as P

EPS = 1e-05
F32 = jnp.float32
BF16 = jnp.bfloat16
VMEM = pltpu.VMEM
ANY = pl.BlockSpec(memory_space=pl.ANY)
OVER_LANES = (((1,), (1,)), ((), ()))


def vspec():
    return pl.BlockSpec(memory_space=VMEM)


def call(body, name, outs, ins, specs, scratch, flops, moved, limit):
    return pl.pallas_call(
        body,
        out_shape=outs,
        in_specs=specs,
        out_specs=jax.tree.map(lambda _: vspec(), outs),
        scratch_shapes=scratch,
        compiler_params=pltpu.CompilerParams(vmem_limit_bytes=limit * 1024 * 1024),
        cost_estimate=pl.CostEstimate(flops=flops, bytes_accessed=moved, transcendentals=0),
        name=name,
    )(*ins)


def chunks_of(extent):
    size = 256 if extent % 256 == 0 else extent
    return [(start, size) for start in range(0, extent, size)]


def wanted_slots(count_ref, picked_ref):
    slots, indices = picked_ref.shape[0], count_ref.shape[0]
    here = lax.broadcasted_iota(jnp.int32, (1, indices), 1) == lax.axis_index("tm")
    count = jnp.sum(jnp.where(here, count_ref[...].reshape(1, indices), 0), axis=1, keepdims=True)
    live = lax.broadcasted_iota(jnp.int32, (8, slots), 1) < count
    wanted = jnp.where(live, jnp.broadcast_to(picked_ref[...].reshape(1, slots), (8, slots)), -1)
    swapped = pltpu.roll(wanted, slots // 2, 1)
    first = lax.axis_index("pair") == 0
    return [jnp.where(first, x, y)[:1, : slots // 2] for x, y in ((wanted, swapped), (swapped, wanted))]


def gather_rows(places, frames):
    onehot = (lax.broadcasted_iota(jnp.int32, (frames.shape[0], 1), 0) == places).astype(BF16)
    return lax.dot_general(onehot, frames, (((0,), (0,)), ((), ())), preferred_element_type=F32).astype(BF16)


def scatter_body(counts, frames_ref, *refs):
    groups, at = [], 0
    for n in counts:
        rows = refs[at + 1][...].astype(F32)
        for ref in refs[at + 2 : at + 1 + n]:
            rows = rows + ref[...].astype(F32)
        groups.append((refs[at][...].reshape(1, refs[at].shape[0]), rows.astype(BF16)))
        at += 1 + n
    out_ref, *scratch = refs[at:]
    stores = []
    for i, (start, size) in enumerate(chunks_of(frames_ref.shape[0])):
        place = lax.broadcasted_iota(jnp.int32, (size, 1), 0) + start
        total = frames_ref[start : start + size, :].astype(F32)
        for wanted, rows in groups:
            onehot = jnp.where(wanted == place, 1.0, 0.0).astype(BF16)
            total = total + jnp.dot(onehot, rows, preferred_element_type=F32)
        if not scratch:
            out_ref[start : start + size, :] = total.astype(BF16)
            continue
        staged, sems = scratch
        staged[start : start + size, :] = total.astype(BF16)
        cut = pl.ds(start, size)
        store = pltpu.make_async_copy(staged.at[cut], out_ref.at[cut], sems.at[i])
        store.start()
        stores.append(store)
    for store in stores:
        store.wait()


def scatter_rows(name, frames, groups, last=True):
    operands = [x for wanted, parts in groups for x in (wanted, *parts)]
    staging = [VMEM(frames.shape, BF16), pltpu.SemaphoreType.DMA((len(chunks_of(frames.shape[0])),))]
    return pl.pallas_call(
        functools.partial(scatter_body, [len(parts) for _, parts in groups]),
        out_shape=jax.ShapeDtypeStruct(frames.shape, BF16),
        in_specs=[vspec()] * (1 + len(operands)),
        out_specs=ANY if last else vspec(),
        scratch_shapes=staging if last else [],
        compiler_params=pltpu.CompilerParams(vmem_limit_bytes=8 * 1024 * 1024),
        name=name,
    )(frames, *operands)


def block_start(step, side, width):
    tensors = lax.axis_size("tensor")
    chip = (lax.axis_index("tensor") + tensors + step) % tensors
    return (chip * 2 + (lax.axis_index("pair") + side) % 2) * width


def assemble(full_ref, blocks, ways, width):
    if len(ways) == 1:
        full_ref[...] = blocks[0][...]
        return
    for (step, side), block in zip(ways, blocks):
        start = pl.multiple_of(block_start(-step, side, width), 128)
        full_ref[:, pl.ds(start, width)] = block[...]


def dissect(total_ref, outs, ways, width):
    if len(ways) == 1:
        outs[0][...] = total_ref[...]
        return
    for (step, side), out in zip(ways, outs):
        start = pl.multiple_of(block_start(step, side, width), 128)
        out[...] = total_ref[:, pl.ds(start, width)]


def forward_body(ways, width, count_ref, picked_ref, *refs):
    n = len(ways)
    blocks = refs[:n]
    up_own, up_sib, down_own, down_sib, gain_ref, router_ref = refs[n : n + 6]
    outs = refs[n + 6 : 2 * n + 6]
    full_ref, stats_ref, hidden_ref, slope_ref = refs[2 * n + 6 : 2 * n + 10]
    mine_ref, sib_ref, total_ref = refs[2 * n + 10 :]
    mine_ref[...], sib_ref[...] = [x.reshape(mine_ref.shape) for x in wanted_slots(count_ref, picked_ref)]
    assemble(full_ref, blocks, ways, width)
    half, features = full_ref.shape
    hidden_dev = up_own.shape[1]
    wide = full_ref[...].astype(F32)
    gate = jax.nn.sigmoid(jnp.sum(wide * router_ref[...].reshape(1, features), axis=1, keepdims=True))
    mean = jnp.sum(wide, axis=1, keepdims=True) * (1.0 / features)
    deviate = wide - mean
    inv = lax.rsqrt(jnp.sum(deviate * deviate, axis=1, keepdims=True) * (1.0 / features) + EPS)
    normed = (deviate * inv * gain_ref[...].reshape(1, features)).astype(BF16)
    lane = lax.broadcasted_iota(jnp.int32, (half, 128), 1)
    stats_ref[...] = jnp.where(lane == 0, mean, jnp.where(lane == 1, inv, gate))
    half_gate = 0.5 * gate
    for i, up in enumerate((up_own, up_sib)):
        value = jnp.dot(normed, up[...], preferred_element_type=F32)
        s = jax.nn.sigmoid(value)
        cols = slice(i * hidden_dev, (i + 1) * hidden_dev)
        hidden_ref[:, cols] = (value * s).astype(BF16)
        slope_ref[:, cols] = half_gate * s * (1.0 + value * (1.0 - s))
    total = jnp.dot(hidden_ref[:, :hidden_dev], down_own[...], preferred_element_type=F32)
    total = total + jnp.dot(hidden_ref[:, hidden_dev:], down_sib[...], preferred_element_type=F32)
    total_ref[...] = (total * half_gate).astype(BF16)
    dissect(total_ref, outs, ways, width)


def forward(count, picked, blocks, ways, weights, gain, router):
    half, width = blocks[0].shape
    features, hidden_dev = weights[0].shape
    piece = jax.ShapeDtypeStruct((half, width), BF16)
    got = call(
        functools.partial(forward_body, ways, width),
        "forward",
        (piece,) * len(ways)
        + (
            jax.ShapeDtypeStruct((half, features), BF16),
            jax.ShapeDtypeStruct((half, 128), F32),
            jax.ShapeDtypeStruct((half, 2 * hidden_dev), BF16),
            jax.ShapeDtypeStruct((half, 2 * hidden_dev), F32),
        )
        + (jax.ShapeDtypeStruct((half,), jnp.int32),) * 2,
        (count, picked, *blocks, *weights, gain, router),
        [vspec()] * (len(blocks) + 8),
        [VMEM((half, features), BF16)],
        1,
        1,
        16,
    )
    return got[: len(ways)], got[len(ways) : -2], got[-2:]


def backward_body(ways, width, *refs):
    n = len(ways)
    blocks = refs[:n]
    up_own, up_sib, down_own, down_sib, gain_ref, router_ref = refs[n : n + 6]
    full_ref, stats_ref, hidden_ref, slope_ref = refs[n + 6 : n + 10]
    outs = refs[n + 10 : 2 * n + 10]
    (cot_ref,) = refs[2 * n + 10 :]
    assemble(cot_ref, blocks, ways, width)
    half, features = full_ref.shape
    hidden_dev = up_own.shape[1]
    score, pre = 0.0, []
    for i, down in enumerate((down_own, down_sib)):
        value = lax.dot_general(cot_ref[...], down[...], OVER_LANES, preferred_element_type=F32)
        cols = slice(i * hidden_dev, (i + 1) * hidden_dev)
        pre.append((value * slope_ref[:, cols]).astype(BF16))
        score = score + jnp.sum(value * hidden_ref[:, cols].astype(F32), axis=1, keepdims=True)
    scaled = lax.dot_general(pre[0], up_own[...], OVER_LANES, preferred_element_type=F32)
    scaled = scaled + lax.dot_general(pre[1], up_sib[...], OVER_LANES, preferred_element_type=F32)
    scaled = scaled * gain_ref[...].reshape(1, features)
    mean, inv, gate = stats_ref[:, 0:1], stats_ref[:, 1:2], stats_ref[:, 2:3]
    centred = (full_ref[...].astype(F32) - mean) * inv
    plain = jnp.sum(scaled, axis=1, keepdims=True) * (1.0 / features)
    cross = jnp.sum(scaled * centred, axis=1, keepdims=True) * (1.0 / features)
    term = 0.5 * score * gate * (1.0 - gate)
    cot_ref[...] = (inv * (scaled - plain - centred * cross) + term * router_ref[...].reshape(1, features)).astype(BF16)
    dissect(cot_ref, outs, ways, width)


def backward(blocks, ways, weights, gain, router, saved):
    half, width = blocks[0].shape
    features, hidden_dev = weights[0].shape
    return call(
        functools.partial(backward_body, ways, width),
        "backward",
        (jax.ShapeDtypeStruct((half, width), BF16),) * len(ways),
        (*blocks, *weights, gain, router, *saved),
        [vspec()] * (len(blocks) + 10),
        [VMEM((half, features), BF16)],
        1,
        1,
        16,
    )


def after(value, *others):
    return lax.optimization_barrier((value, *others))[0]


def per_device(frames, router_weight, norm_gain, up_weight, down_weight, picked_rows, picked_count, cotangent):
    width = frames.shape[1]
    features = up_weight.shape[0]
    half = picked_rows.shape[0] // 2
    tensors = lax.axis_size("tensor")
    gain, router = norm_gain, router_weight
    steps = range(1, tensors)
    aligned = width % 128 == 0
    pieces = [(0, 0), (0, 1)] + [(k, 0) for k in steps] + [(k, 1) for k in steps]
    ways = pieces if aligned else [(0, 0)]

    def send(x, k, side):
        pairs = [
            (chip * 2 + core, (chip + k) % tensors * 2 + (core + side) % 2) for chip in range(tensors) for core in (0, 1)
        ]
        return lax.ppermute(x, ("tensor", "pair"), pairs)

    def swap(x):
        return lax.ppermute(x, "pair", [(0, 1), (1, 0)])

    def joined(blocks):
        if aligned:
            return blocks
        full = jnp.zeros((half, features), BF16)
        for (k, side), block in zip(pieces, blocks):
            full = lax.dynamic_update_slice_in_dim(full, block, block_start(-k, side, width), 1)
        return [full]

    def cut(outs):
        if aligned:
            return outs
        return [lax.dynamic_slice_in_dim(outs[0], block_start(k, side, width), width, 1) for k, side in pieces]

    def collect(mine, sib, near):
        return [mine, swap(near)] + [send(mine, k, 0) for k in steps] + [send(sib, k, 1) for k in steps]

    def deliver(parts):
        count = tensors - 1
        far_mine = [send(x, k, 0) for x, k in zip(parts[2 : 2 + count], steps)]
        far_sib = [send(x, k, 1) for x, k in zip(parts[2 + count :], steps)]
        return [parts[0]] + far_mine, [swap(parts[1])] + far_sib

    first = lax.axis_index("pair") == 0
    places_mine = jnp.where(first, picked_rows[:half], picked_rows[half:])
    places_sib = jnp.where(first, picked_rows[half:], picked_rows[:half])
    found = (lax.broadcasted_iota(jnp.int32, (frames.shape[0], 1), 0) == picked_rows).astype(BF16)
    rows = lax.dot_general(found, frames, (((0,), (0,)), ((), ())), preferred_element_type=F32).astype(BF16)
    mine = jnp.where(first, rows[:half], rows[half:])
    sib = jnp.where(first, rows[half:], rows[:half])
    blocks = collect(mine, sib, after(sib, mine))
    up_sib, down_sib = swap(up_weight), swap(after(down_weight, mine))
    weights = (up_weight, up_sib, down_weight, down_sib)
    rows = lax.dot_general(found, cotangent, (((0,), (0,)), ((), ())), preferred_element_type=F32).astype(BF16)
    cot_mine = jnp.where(first, rows[:half], rows[half:])
    cot_sib = jnp.where(first, rows[half:], rows[:half])
    cot_mine, cot_sib = after(cot_mine, up_sib), after(cot_sib, up_sib, blocks[1])
    cot_blocks = collect(cot_mine, cot_sib, cot_sib)
    parts, saved, wanted = forward(picked_count, picked_rows, joined(blocks), ways, weights, gain, router)
    out_mine, out_sib = deliver(cut(parts))
    grads = backward(joined(cot_blocks), ways, weights, gain, router, saved)
    grad_mine, grad_sib = deliver(cut(grads))
    mixed = scatter_rows("mixed_rows", frames, [(wanted[0], out_mine), (wanted[1], out_sib)])
    grad_mine[0] = after(grad_mine[0], mixed)
    started = scatter_rows("grad_rows_mine", cotangent, [(wanted[0], grad_mine)], last=False)
    frames_grad = scatter_rows("grad_rows", started, [(wanted[1], grad_sib)])
    return (mixed, frames_grad)


def solution(mesh):
    return jax.shard_map(
        per_device,
        mesh=mesh,
        in_specs=(
            P(("group", "tm"), ("tensor", "pair")),
            P(),
            P(),
            P(None, ("tensor", "pair")),
            P(("tensor", "pair"), None),
            P(("group", "tm")),
            P("group"),
            P(("group", "tm"), ("tensor", "pair")),
        ),
        out_specs=(P(("group", "tm"), ("tensor", "pair")), P(("group", "tm"), ("tensor", "pair"))),
        check_vma=False,
    )
```

```python
import functools

import jax
import jax.numpy as jnp
from jax import lax
from jax.experimental import pallas as pl
from jax.experimental.pallas import tpu as pltpu
from jax.sharding import PartitionSpec as P

EPS = 1e-05
F32 = jnp.float32
BF16 = jnp.bfloat16
VMEM = pltpu.VMEM
ANY = pl.BlockSpec(memory_space=pl.ANY)
OVER_LANES = (((1,), (1,)), ((), ()))


def vspec():
    return pl.BlockSpec(memory_space=VMEM)


def call(body, name, outs, ins, specs, scratch, flops, moved, limit):
    return pl.pallas_call(
        body,
        out_shape=outs,
        in_specs=specs,
        out_specs=jax.tree.map(lambda _: vspec(), outs),
        scratch_shapes=scratch,
        compiler_params=pltpu.CompilerParams(vmem_limit_bytes=limit * 1024 * 1024),
        cost_estimate=pl.CostEstimate(flops=flops, bytes_accessed=moved, transcendentals=0),
        name=name,
    )(*ins)


def chunks_of(extent):
    if extent % 256:
        return [(0, extent)]
    sizes = [64, 192] + [256] * (extent // 256 - 1)
    return [(sum(sizes[:i]), size) for i, size in enumerate(sizes)]


def wanted_slots(count_ref, picked_ref):
    slots, indices = picked_ref.shape[0], count_ref.shape[0]
    here = lax.broadcasted_iota(jnp.int32, (1, indices), 1) == lax.axis_index("tm")
    count = jnp.sum(jnp.where(here, count_ref[...].reshape(1, indices), 0), axis=1, keepdims=True)
    live = lax.broadcasted_iota(jnp.int32, (8, slots), 1) < count
    wanted = jnp.where(live, jnp.broadcast_to(picked_ref[...].reshape(1, slots), (8, slots)), -1)
    swapped = pltpu.roll(wanted, slots // 2, 1)
    first = lax.axis_index("pair") == 0
    return [jnp.where(first, x, y)[:1, : slots // 2] for x, y in ((wanted, swapped), (swapped, wanted))]


def gather_rows(places, frames):
    onehot = (lax.broadcasted_iota(jnp.int32, (frames.shape[0], 1), 0) == places).astype(BF16)
    return lax.dot_general(onehot, frames, (((0,), (0,)), ((), ())), preferred_element_type=F32).astype(BF16)


def scatter_body(counts, frames_ref, *refs):
    groups, at = [], 0
    for n in counts:
        rows = refs[at + 1][...].astype(F32)
        for ref in refs[at + 2 : at + 1 + n]:
            rows = rows + ref[...].astype(F32)
        groups.append((refs[at][...].reshape(1, refs[at].shape[0]), rows.astype(BF16)))
        at += 1 + n
    out_ref, *scratch = refs[at:]
    stores = []
    for i, (start, size) in enumerate(chunks_of(frames_ref.shape[0])):
        place = lax.broadcasted_iota(jnp.int32, (size, 1), 0) + start
        total = frames_ref[start : start + size, :].astype(F32)
        for wanted, rows in groups:
            onehot = jnp.where(wanted == place, 1.0, 0.0).astype(BF16)
            total = total + jnp.dot(onehot, rows, preferred_element_type=F32)
        if not scratch:
            out_ref[start : start + size, :] = total.astype(BF16)
            continue
        staged, sems = scratch
        staged[start : start + size, :] = total.astype(BF16)
        cut = pl.ds(start, size)
        store = pltpu.make_async_copy(staged.at[cut], out_ref.at[cut], sems.at[i])
        store.start()
        stores.append(store)
    for store in stores:
        store.wait()


def scatter_rows(name, frames, groups, last=True):
    operands = [x for wanted, parts in groups for x in (wanted, *parts)]
    staging = [VMEM(frames.shape, BF16), pltpu.SemaphoreType.DMA((len(chunks_of(frames.shape[0])),))]
    return pl.pallas_call(
        functools.partial(scatter_body, [len(parts) for _, parts in groups]),
        out_shape=jax.ShapeDtypeStruct(frames.shape, BF16),
        in_specs=[vspec()] * (1 + len(operands)),
        out_specs=ANY if last else vspec(),
        scratch_shapes=staging if last else [],
        compiler_params=pltpu.CompilerParams(vmem_limit_bytes=8 * 1024 * 1024),
        name=name,
    )(frames, *operands)


def block_start(step, side, width):
    tensors = lax.axis_size("tensor")
    chip = (lax.axis_index("tensor") + tensors + step) % tensors
    return (chip * 2 + (lax.axis_index("pair") + side) % 2) * width


def assemble(full_ref, blocks, ways, width):
    if len(ways) == 1:
        full_ref[...] = blocks[0][...]
        return
    for (step, side), block in zip(ways, blocks):
        start = pl.multiple_of(block_start(-step, side, width), 128)
        full_ref[:, pl.ds(start, width)] = block[...]


def dissect(total_ref, outs, ways, width):
    if len(ways) == 1:
        outs[0][...] = total_ref[...]
        return
    for (step, side), out in zip(ways, outs):
        start = pl.multiple_of(block_start(step, side, width), 128)
        out[...] = total_ref[:, pl.ds(start, width)]


def forward_body(ways, width, count_ref, picked_ref, *refs):
    n = len(ways)
    blocks = refs[:n]
    up_own, up_sib, down_own, down_sib, gain_ref, router_ref = refs[n : n + 6]
    outs = refs[n + 6 : 2 * n + 6]
    full_ref, stats_ref, hidden_ref, slope_ref = refs[2 * n + 6 : 2 * n + 10]
    mine_ref, sib_ref, total_ref = refs[2 * n + 10 :]
    mine_ref[...], sib_ref[...] = [x.reshape(mine_ref.shape) for x in wanted_slots(count_ref, picked_ref)]
    assemble(full_ref, blocks, ways, width)
    half, features = full_ref.shape
    hidden_dev = up_own.shape[1]
    wide = full_ref[...].astype(F32)
    gate = jax.nn.sigmoid(jnp.sum(wide * router_ref[...].reshape(1, features), axis=1, keepdims=True))
    mean = jnp.sum(wide, axis=1, keepdims=True) * (1.0 / features)
    deviate = wide - mean
    inv = lax.rsqrt(jnp.sum(deviate * deviate, axis=1, keepdims=True) * (1.0 / features) + EPS)
    normed = (deviate * inv * gain_ref[...].reshape(1, features)).astype(BF16)
    lane = lax.broadcasted_iota(jnp.int32, (half, 128), 1)
    stats_ref[...] = jnp.where(lane == 0, mean, jnp.where(lane == 1, inv, gate))
    half_gate = 0.5 * gate
    for i, up in enumerate((up_own, up_sib)):
        value = jnp.dot(normed, up[...], preferred_element_type=F32)
        s = jax.nn.sigmoid(value)
        cols = slice(i * hidden_dev, (i + 1) * hidden_dev)
        hidden_ref[:, cols] = (value * s).astype(BF16)
        slope_ref[:, cols] = half_gate * s * (1.0 + value * (1.0 - s))
    total = jnp.dot(hidden_ref[:, :hidden_dev], down_own[...], preferred_element_type=F32)
    total = total + jnp.dot(hidden_ref[:, hidden_dev:], down_sib[...], preferred_element_type=F32)
    total_ref[...] = (total * half_gate).astype(BF16)
    dissect(total_ref, outs, ways, width)


def forward(count, picked, blocks, ways, weights, gain, router):
    half, width = blocks[0].shape
    features, hidden_dev = weights[0].shape
    piece = jax.ShapeDtypeStruct((half, width), BF16)
    got = call(
        functools.partial(forward_body, ways, width),
        "forward",
        (piece,) * len(ways)
        + (
            jax.ShapeDtypeStruct((half, features), BF16),
            jax.ShapeDtypeStruct((half, 128), F32),
            jax.ShapeDtypeStruct((half, 2 * hidden_dev), BF16),
            jax.ShapeDtypeStruct((half, 2 * hidden_dev), F32),
        )
        + (jax.ShapeDtypeStruct((half,), jnp.int32),) * 2,
        (count, picked, *blocks, *weights, gain, router),
        [vspec()] * (len(blocks) + 8),
        [VMEM((half, features), BF16)],
        1,
        1,
        16,
    )
    return got[: len(ways)], got[len(ways) : -2], got[-2:]


def backward_body(ways, width, *refs):
    n = len(ways)
    blocks = refs[:n]
    up_own, up_sib, down_own, down_sib, gain_ref, router_ref = refs[n : n + 6]
    full_ref, stats_ref, hidden_ref, slope_ref = refs[n + 6 : n + 10]
    outs = refs[n + 10 : 2 * n + 10]
    (cot_ref,) = refs[2 * n + 10 :]
    assemble(cot_ref, blocks, ways, width)
    half, features = full_ref.shape
    hidden_dev = up_own.shape[1]
    score, pre = 0.0, []
    for i, down in enumerate((down_own, down_sib)):
        value = lax.dot_general(cot_ref[...], down[...], OVER_LANES, preferred_element_type=F32)
        cols = slice(i * hidden_dev, (i + 1) * hidden_dev)
        pre.append((value * slope_ref[:, cols]).astype(BF16))
        score = score + jnp.sum(value * hidden_ref[:, cols].astype(F32), axis=1, keepdims=True)
    scaled = lax.dot_general(pre[0], up_own[...], OVER_LANES, preferred_element_type=F32)
    scaled = scaled + lax.dot_general(pre[1], up_sib[...], OVER_LANES, preferred_element_type=F32)
    scaled = scaled * gain_ref[...].reshape(1, features)
    mean, inv, gate = stats_ref[:, 0:1], stats_ref[:, 1:2], stats_ref[:, 2:3]
    centred = (full_ref[...].astype(F32) - mean) * inv
    plain = jnp.sum(scaled, axis=1, keepdims=True) * (1.0 / features)
    cross = jnp.sum(scaled * centred, axis=1, keepdims=True) * (1.0 / features)
    term = 0.5 * score * gate * (1.0 - gate)
    cot_ref[...] = (inv * (scaled - plain - centred * cross) + term * router_ref[...].reshape(1, features)).astype(BF16)
    dissect(cot_ref, outs, ways, width)


def backward(blocks, ways, weights, gain, router, saved):
    half, width = blocks[0].shape
    features, hidden_dev = weights[0].shape
    return call(
        functools.partial(backward_body, ways, width),
        "backward",
        (jax.ShapeDtypeStruct((half, width), BF16),) * len(ways),
        (*blocks, *weights, gain, router, *saved),
        [vspec()] * (len(blocks) + 10),
        [VMEM((half, features), BF16)],
        1,
        1,
        16,
    )


def after(value, *others):
    return lax.optimization_barrier((value, *others))[0]


def per_device(frames, router_weight, norm_gain, up_weight, down_weight, picked_rows, picked_count, cotangent):
    width = frames.shape[1]
    features = up_weight.shape[0]
    half = picked_rows.shape[0] // 2
    tensors = lax.axis_size("tensor")
    gain, router = norm_gain, router_weight
    steps = range(1, tensors)
    aligned = width % 128 == 0
    pieces = [(0, 0), (0, 1)] + [(k, 0) for k in steps] + [(k, 1) for k in steps]
    ways = pieces if aligned else [(0, 0)]

    def send(x, k, side):
        pairs = [
            (chip * 2 + core, (chip + k) % tensors * 2 + (core + side) % 2) for chip in range(tensors) for core in (0, 1)
        ]
        return lax.ppermute(x, ("tensor", "pair"), pairs)

    def swap(x):
        return lax.ppermute(x, "pair", [(0, 1), (1, 0)])

    def joined(blocks):
        if aligned:
            return blocks
        full = jnp.zeros((half, features), BF16)
        for (k, side), block in zip(pieces, blocks):
            full = lax.dynamic_update_slice_in_dim(full, block, block_start(-k, side, width), 1)
        return [full]

    def cut(outs):
        if aligned:
            return outs
        return [lax.dynamic_slice_in_dim(outs[0], block_start(k, side, width), width, 1) for k, side in pieces]

    def collect(mine, sib, near):
        return [mine, swap(near)] + [send(mine, k, 0) for k in steps] + [send(sib, k, 1) for k in steps]

    def deliver(parts):
        count = tensors - 1
        far_mine = [send(x, k, 0) for x, k in zip(parts[2 : 2 + count], steps)]
        far_sib = [send(x, k, 1) for x, k in zip(parts[2 + count :], steps)]
        return [parts[0]] + far_mine, [swap(parts[1])] + far_sib

    first = lax.axis_index("pair") == 0
    places_mine = jnp.where(first, picked_rows[:half], picked_rows[half:])
    places_sib = jnp.where(first, picked_rows[half:], picked_rows[:half])
    found = (lax.broadcasted_iota(jnp.int32, (frames.shape[0], 1), 0) == picked_rows).astype(BF16)
    rows = lax.dot_general(found, frames, (((0,), (0,)), ((), ())), preferred_element_type=F32).astype(BF16)
    mine = jnp.where(first, rows[:half], rows[half:])
    sib = jnp.where(first, rows[half:], rows[:half])
    blocks = collect(mine, sib, after(sib, mine))
    up_sib, down_sib = swap(up_weight), swap(after(down_weight, mine))
    weights = (up_weight, up_sib, down_weight, down_sib)
    rows = lax.dot_general(found, cotangent, (((0,), (0,)), ((), ())), preferred_element_type=F32).astype(BF16)
    cot_mine = jnp.where(first, rows[:half], rows[half:])
    cot_sib = jnp.where(first, rows[half:], rows[:half])
    cot_mine, cot_sib = after(cot_mine, up_sib), after(cot_sib, up_sib, blocks[1])
    cot_blocks = collect(cot_mine, cot_sib, cot_sib)
    parts, saved, wanted = forward(picked_count, picked_rows, joined(blocks), ways, weights, gain, router)
    out_mine, out_sib = deliver(cut(parts))
    grads = backward(joined(cot_blocks), ways, weights, gain, router, saved)
    grad_mine, grad_sib = deliver(cut(grads))
    mixed = scatter_rows("mixed_rows", frames, [(wanted[0], out_mine), (wanted[1], out_sib)])
    grad_mine[0] = after(grad_mine[0], mixed)
    started = scatter_rows("grad_rows_mine", cotangent, [(wanted[0], grad_mine)], last=False)
    frames_grad = scatter_rows("grad_rows", started, [(wanted[1], grad_sib)])
    return (mixed, frames_grad)


def solution(mesh):
    return jax.shard_map(
        per_device,
        mesh=mesh,
        in_specs=(
            P(("group", "tm"), ("tensor", "pair")),
            P(),
            P(),
            P(None, ("tensor", "pair")),
            P(("tensor", "pair"), None),
            P(("group", "tm")),
            P("group"),
            P(("group", "tm"), ("tensor", "pair")),
        ),
        out_specs=(P(("group", "tm"), ("tensor", "pair")), P(("group", "tm"), ("tensor", "pair"))),
        check_vma=False,
    )
```

```python
import functools

import jax
import jax.numpy as jnp
from jax import lax
from jax.experimental import pallas as pl
from jax.experimental.pallas import tpu as pltpu
from jax.sharding import PartitionSpec as P

EPS = 1e-05
F32 = jnp.float32
BF16 = jnp.bfloat16
VMEM = pltpu.VMEM
ANY = pl.BlockSpec(memory_space=pl.ANY)
OVER_LANES = (((1,), (1,)), ((), ()))


def vspec():
    return pl.BlockSpec(memory_space=VMEM)


def call(body, name, outs, ins, specs, scratch, flops, moved, limit):
    return pl.pallas_call(
        body,
        out_shape=outs,
        in_specs=specs,
        out_specs=jax.tree.map(lambda _: vspec(), outs),
        scratch_shapes=scratch,
        compiler_params=pltpu.CompilerParams(vmem_limit_bytes=limit * 1024 * 1024),
        cost_estimate=pl.CostEstimate(flops=flops, bytes_accessed=moved, transcendentals=0),
        name=name,
    )(*ins)


def chunks_of(extent):
    size = 256 if extent % 256 == 0 else extent
    return [(start, size) for start in range(0, extent, size)]


def wanted_slots(count_ref, picked_ref):
    slots, indices = picked_ref.shape[0], count_ref.shape[0]
    here = lax.broadcasted_iota(jnp.int32, (1, indices), 1) == lax.axis_index("tm")
    count = jnp.sum(jnp.where(here, count_ref[...].reshape(1, indices), 0), axis=1, keepdims=True)
    live = lax.broadcasted_iota(jnp.int32, (8, slots), 1) < count
    wanted = jnp.where(live, jnp.broadcast_to(picked_ref[...].reshape(1, slots), (8, slots)), -1)
    swapped = pltpu.roll(wanted, slots // 2, 1)
    first = lax.axis_index("pair") == 0
    return [jnp.where(first, x, y)[:1, : slots // 2] for x, y in ((wanted, swapped), (swapped, wanted))]


def gather_rows(places, frames):
    onehot = (lax.broadcasted_iota(jnp.int32, (frames.shape[0], 1), 0) == places).astype(BF16)
    return lax.dot_general(onehot, frames, (((0,), (0,)), ((), ())), preferred_element_type=F32).astype(BF16)


def scatter_body(counts, frames_ref, *refs):
    groups, at = [], 0
    for n in counts:
        rows = refs[at + 1][...].astype(F32)
        for ref in refs[at + 2 : at + 1 + n]:
            rows = rows + ref[...].astype(F32)
        groups.append((refs[at][...].reshape(1, refs[at].shape[0]), rows.astype(BF16)))
        at += 1 + n
    out_ref, *scratch = refs[at:]
    stores = []
    for i, (start, size) in enumerate(chunks_of(frames_ref.shape[0])):
        place = lax.broadcasted_iota(jnp.int32, (size, 1), 0) + start
        total = frames_ref[start : start + size, :].astype(F32)
        for wanted, rows in groups:
            onehot = jnp.where(wanted == place, 1.0, 0.0).astype(BF16)
            total = total + jnp.dot(onehot, rows, preferred_element_type=F32)
        if not scratch:
            out_ref[start : start + size, :] = total.astype(BF16)
            continue
        staged, sems = scratch
        staged[start : start + size, :] = total.astype(BF16)
        cut = pl.ds(start, size)
        store = pltpu.make_async_copy(staged.at[cut], out_ref.at[cut], sems.at[i])
        store.start()
        stores.append(store)
    for store in stores:
        store.wait()


def scatter_rows(name, frames, groups, last=True):
    operands = [x for wanted, parts in groups for x in (wanted, *parts)]
    staging = [VMEM(frames.shape, BF16), pltpu.SemaphoreType.DMA((len(chunks_of(frames.shape[0])),))]
    return pl.pallas_call(
        functools.partial(scatter_body, [len(parts) for _, parts in groups]),
        out_shape=jax.ShapeDtypeStruct(frames.shape, BF16),
        in_specs=[vspec()] * (1 + len(operands)),
        out_specs=ANY if last else vspec(),
        scratch_shapes=staging if last else [],
        compiler_params=pltpu.CompilerParams(vmem_limit_bytes=8 * 1024 * 1024),
        name=name,
    )(frames, *operands)


def block_start(step, side, width):
    tensors = lax.axis_size("tensor")
    chip = (lax.axis_index("tensor") + tensors + step) % tensors
    return (chip * 2 + (lax.axis_index("pair") + side) % 2) * width


def assemble(full_ref, blocks, ways, width):
    if len(ways) == 1:
        full_ref[...] = blocks[0][...]
        return
    for (step, side), block in zip(ways, blocks):
        start = pl.multiple_of(block_start(-step, side, width), 128)
        full_ref[:, pl.ds(start, width)] = block[...]


def dissect(total_ref, outs, ways, width):
    if len(ways) == 1:
        outs[0][...] = total_ref[...]
        return
    for (step, side), out in zip(ways, outs):
        start = pl.multiple_of(block_start(step, side, width), 128)
        out[...] = total_ref[:, pl.ds(start, width)]


def forward_body(ways, width, count_ref, picked_ref, *refs):
    n = len(ways)
    blocks = refs[:n]
    up_own, up_sib, down_own, down_sib, gain_ref, router_ref = refs[n : n + 6]
    outs = refs[n + 6 : 2 * n + 6]
    full_ref, stats_ref, hidden_ref, slope_ref = refs[2 * n + 6 : 2 * n + 10]
    mine_ref, sib_ref, total_ref = refs[2 * n + 10 :]
    mine_ref[...], sib_ref[...] = [x.reshape(mine_ref.shape) for x in wanted_slots(count_ref, picked_ref)]
    assemble(full_ref, blocks, ways, width)
    half, features = full_ref.shape
    hidden_dev = up_own.shape[1]
    wide = full_ref[...].astype(F32)
    gate = jax.nn.sigmoid(jnp.sum(wide * router_ref[...].reshape(1, features), axis=1, keepdims=True))
    mean = jnp.sum(wide, axis=1, keepdims=True) * (1.0 / features)
    deviate = wide - mean
    inv = lax.rsqrt(jnp.sum(deviate * deviate, axis=1, keepdims=True) * (1.0 / features) + EPS)
    normed = (deviate * inv * gain_ref[...].reshape(1, features)).astype(BF16)
    lane = lax.broadcasted_iota(jnp.int32, (half, 128), 1)
    stats_ref[...] = jnp.where(lane == 0, mean, jnp.where(lane == 1, inv, gate))
    half_gate = 0.5 * gate
    for i, up in enumerate((up_own, up_sib)):
        value = jnp.dot(normed, up[...], preferred_element_type=F32)
        s = jax.nn.sigmoid(value)
        cols = slice(i * hidden_dev, (i + 1) * hidden_dev)
        hidden_ref[:, cols] = (value * s).astype(BF16)
        slope_ref[:, cols] = half_gate * s * (1.0 + value * (1.0 - s))
    total = jnp.dot(hidden_ref[:, :hidden_dev], down_own[...], preferred_element_type=F32)
    total = total + jnp.dot(hidden_ref[:, hidden_dev:], down_sib[...], preferred_element_type=F32)
    total_ref[...] = (total * half_gate).astype(BF16)
    dissect(total_ref, outs, ways, width)


def forward(count, picked, blocks, ways, weights, gain, router):
    half, width = blocks[0].shape
    features, hidden_dev = weights[0].shape
    piece = jax.ShapeDtypeStruct((half, width), BF16)
    got = call(
        functools.partial(forward_body, ways, width),
        "forward",
        (piece,) * len(ways)
        + (
            jax.ShapeDtypeStruct((half, features), BF16),
            jax.ShapeDtypeStruct((half, 128), F32),
            jax.ShapeDtypeStruct((half, 2 * hidden_dev), BF16),
            jax.ShapeDtypeStruct((half, 2 * hidden_dev), F32),
        )
        + (jax.ShapeDtypeStruct((half,), jnp.int32),) * 2,
        (count, picked, *blocks, *weights, gain, router),
        [vspec()] * (len(blocks) + 8),
        [VMEM((half, features), BF16)],
        1,
        1,
        16,
    )
    return got[: len(ways)], got[len(ways) : -2], got[-2:]


def backward_body(ways, width, *refs):
    n = len(ways)
    blocks = refs[:n]
    up_own, up_sib, down_own, down_sib, gain_ref, router_ref = refs[n : n + 6]
    full_ref, stats_ref, hidden_ref, slope_ref = refs[n + 6 : n + 10]
    outs = refs[n + 10 : 2 * n + 10]
    (cot_ref,) = refs[2 * n + 10 :]
    assemble(cot_ref, blocks, ways, width)
    half, features = full_ref.shape
    hidden_dev = up_own.shape[1]
    score, pre = 0.0, []
    for i, down in enumerate((down_own, down_sib)):
        value = lax.dot_general(cot_ref[...], down[...], OVER_LANES, preferred_element_type=F32)
        cols = slice(i * hidden_dev, (i + 1) * hidden_dev)
        pre.append((value * slope_ref[:, cols]).astype(BF16))
        score = score + jnp.sum(value * hidden_ref[:, cols].astype(F32), axis=1, keepdims=True)
    scaled = lax.dot_general(pre[0], up_own[...], OVER_LANES, preferred_element_type=F32)
    scaled = scaled + lax.dot_general(pre[1], up_sib[...], OVER_LANES, preferred_element_type=F32)
    scaled = scaled * gain_ref[...].reshape(1, features)
    mean, inv, gate = stats_ref[:, 0:1], stats_ref[:, 1:2], stats_ref[:, 2:3]
    centred = (full_ref[...].astype(F32) - mean) * inv
    plain = jnp.sum(scaled, axis=1, keepdims=True) * (1.0 / features)
    cross = jnp.sum(scaled * centred, axis=1, keepdims=True) * (1.0 / features)
    term = 0.5 * score * gate * (1.0 - gate)
    cot_ref[...] = (inv * (scaled - plain - centred * cross) + term * router_ref[...].reshape(1, features)).astype(BF16)
    dissect(cot_ref, outs, ways, width)


def backward(blocks, ways, weights, gain, router, saved):
    half, width = blocks[0].shape
    features, hidden_dev = weights[0].shape
    return call(
        functools.partial(backward_body, ways, width),
        "backward",
        (jax.ShapeDtypeStruct((half, width), BF16),) * len(ways),
        (*blocks, *weights, gain, router, *saved),
        [vspec()] * (len(blocks) + 10),
        [VMEM((half, features), BF16)],
        1,
        1,
        16,
    )


def in_vmem(x):
    def body(source, target, sem):
        copy = pltpu.make_async_copy(source, target, sem)
        copy.start()
        copy.wait()

    return pl.pallas_call(
        body,
        out_shape=jax.ShapeDtypeStruct(x.shape, x.dtype),
        in_specs=[ANY],
        out_specs=vspec(),
        scratch_shapes=[pltpu.SemaphoreType.DMA],
        compiler_params=pltpu.CompilerParams(vmem_limit_bytes=6 * 1024 * 1024),
        name="in_vmem",
    )(x)


def after(value, *others):
    return lax.optimization_barrier((value, *others))[0]


def per_device(frames, router_weight, norm_gain, up_weight, down_weight, picked_rows, picked_count, cotangent):
    width = frames.shape[1]
    features = up_weight.shape[0]
    half = picked_rows.shape[0] // 2
    tensors = lax.axis_size("tensor")
    gain, router = norm_gain, router_weight
    steps = range(1, tensors)
    aligned = width % 128 == 0
    pieces = [(0, 0), (0, 1)] + [(k, 0) for k in steps] + [(k, 1) for k in steps]
    ways = pieces if aligned else [(0, 0)]

    def send(x, k, side):
        pairs = [
            (chip * 2 + core, (chip + k) % tensors * 2 + (core + side) % 2) for chip in range(tensors) for core in (0, 1)
        ]
        return lax.ppermute(x, ("tensor", "pair"), pairs)

    def swap(x):
        return lax.ppermute(x, "pair", [(0, 1), (1, 0)])

    def joined(blocks):
        if aligned:
            return blocks
        full = jnp.zeros((half, features), BF16)
        for (k, side), block in zip(pieces, blocks):
            full = lax.dynamic_update_slice_in_dim(full, block, block_start(-k, side, width), 1)
        return [full]

    def cut(outs):
        if aligned:
            return outs
        return [lax.dynamic_slice_in_dim(outs[0], block_start(k, side, width), width, 1) for k, side in pieces]

    def collect(mine, sib, near):
        return [mine, swap(near)] + [send(mine, k, 0) for k in steps] + [send(sib, k, 1) for k in steps]

    def deliver(parts):
        count = tensors - 1
        far_mine = [send(x, k, 0) for x, k in zip(parts[2 : 2 + count], steps)]
        far_sib = [send(x, k, 1) for x, k in zip(parts[2 + count :], steps)]
        return [parts[0]] + far_mine, [swap(parts[1])] + far_sib

    first = lax.axis_index("pair") == 0
    places_mine = jnp.where(first, picked_rows[:half], picked_rows[half:])
    places_sib = jnp.where(first, picked_rows[half:], picked_rows[:half])
    found = (lax.broadcasted_iota(jnp.int32, (frames.shape[0], 1), 0) == picked_rows).astype(BF16)
    rows = lax.dot_general(found, frames, (((0,), (0,)), ((), ())), preferred_element_type=F32).astype(BF16)
    mine = jnp.where(first, rows[:half], rows[half:])
    sib = jnp.where(first, rows[half:], rows[:half])
    blocks = collect(mine, sib, after(sib, mine))
    up_sib, down_sib = swap(up_weight), in_vmem(swap(down_weight))
    weights = (up_weight, up_sib, down_weight, down_sib)
    rows = lax.dot_general(found, cotangent, (((0,), (0,)), ((), ())), preferred_element_type=F32).astype(BF16)
    cot_mine = jnp.where(first, rows[:half], rows[half:])
    cot_sib = jnp.where(first, rows[half:], rows[:half])
    cot_mine, cot_sib = after(cot_mine, up_sib), after(cot_sib, up_sib, blocks[1])
    cot_blocks = collect(cot_mine, cot_sib, after(cot_sib, down_sib))
    parts, saved, wanted = forward(picked_count, picked_rows, joined(blocks), ways, weights, gain, router)
    out_mine, out_sib = deliver(cut(parts))
    grads = backward(joined(cot_blocks), ways, weights, gain, router, saved)
    grad_mine, grad_sib = deliver(cut(grads))
    mixed = scatter_rows("mixed_rows", frames, [(wanted[0], out_mine), (wanted[1], out_sib)])
    grad_mine[0] = after(grad_mine[0], mixed)
    started = scatter_rows("grad_rows_mine", cotangent, [(wanted[0], grad_mine)], last=False)
    frames_grad = scatter_rows("grad_rows", started, [(wanted[1], grad_sib)])
    return (mixed, frames_grad)


def solution(mesh):
    return jax.shard_map(
        per_device,
        mesh=mesh,
        in_specs=(
            P(("group", "tm"), ("tensor", "pair")),
            P(),
            P(),
            P(None, ("tensor", "pair")),
            P(("tensor", "pair"), None),
            P(("group", "tm")),
            P("group"),
            P(("group", "tm"), ("tensor", "pair")),
        ),
        out_specs=(P(("group", "tm"), ("tensor", "pair")), P(("group", "tm"), ("tensor", "pair"))),
        check_vma=False,
    )
```

```python
import functools

import jax
import jax.numpy as jnp
from jax import lax
from jax.experimental import pallas as pl
from jax.experimental.pallas import tpu as pltpu
from jax.sharding import PartitionSpec as P

EPS = 1e-05
F32 = jnp.float32
BF16 = jnp.bfloat16
VMEM = pltpu.VMEM
ANY = pl.BlockSpec(memory_space=pl.ANY)
OVER_LANES = (((1,), (1,)), ((), ()))


def vspec():
    return pl.BlockSpec(memory_space=VMEM)


def call(body, name, outs, ins, specs, scratch, flops, moved, limit):
    return pl.pallas_call(
        body,
        out_shape=outs,
        in_specs=specs,
        out_specs=jax.tree.map(lambda _: vspec(), outs),
        scratch_shapes=scratch,
        compiler_params=pltpu.CompilerParams(vmem_limit_bytes=limit * 1024 * 1024),
        cost_estimate=pl.CostEstimate(flops=flops, bytes_accessed=moved, transcendentals=0),
        name=name,
    )(*ins)


def chunks_of(extent):
    size = 256 if extent % 256 == 0 else extent
    return [(start, size) for start in range(0, extent, size)]


def wanted_slots(count_ref, picked_ref):
    slots, indices = picked_ref.shape[0], count_ref.shape[0]
    here = lax.broadcasted_iota(jnp.int32, (1, indices), 1) == lax.axis_index("tm")
    count = jnp.sum(jnp.where(here, count_ref[...].reshape(1, indices), 0), axis=1, keepdims=True)
    live = lax.broadcasted_iota(jnp.int32, (8, slots), 1) < count
    wanted = jnp.where(live, jnp.broadcast_to(picked_ref[...].reshape(1, slots), (8, slots)), -1)
    swapped = pltpu.roll(wanted, slots // 2, 1)
    first = lax.axis_index("pair") == 0
    return [jnp.where(first, x, y)[:1, : slots // 2] for x, y in ((wanted, swapped), (swapped, wanted))]


def gather_rows(places, frames):
    onehot = (lax.broadcasted_iota(jnp.int32, (frames.shape[0], 1), 0) == places).astype(BF16)
    return lax.dot_general(onehot, frames, (((0,), (0,)), ((), ())), preferred_element_type=F32).astype(BF16)


def scatter_body(counts, frames_ref, *refs):
    groups, at = [], 0
    for n in counts:
        rows = refs[at + 1][...].astype(F32)
        for ref in refs[at + 2 : at + 1 + n]:
            rows = rows + ref[...].astype(F32)
        groups.append((refs[at][...].reshape(1, refs[at].shape[0]), rows.astype(BF16)))
        at += 1 + n
    out_ref, *scratch = refs[at:]
    stores = []
    for i, (start, size) in enumerate(chunks_of(frames_ref.shape[0])):
        place = lax.broadcasted_iota(jnp.int32, (size, 1), 0) + start
        total = frames_ref[start : start + size, :].astype(F32)
        for wanted, rows in groups:
            onehot = jnp.where(wanted == place, 1.0, 0.0).astype(BF16)
            total = total + jnp.dot(onehot, rows, preferred_element_type=F32)
        if not scratch:
            out_ref[start : start + size, :] = total.astype(BF16)
            continue
        staged, sems = scratch
        staged[start : start + size, :] = total.astype(BF16)
        cut = pl.ds(start, size)
        store = pltpu.make_async_copy(staged.at[cut], out_ref.at[cut], sems.at[i])
        store.start()
        stores.append(store)
    for store in stores:
        store.wait()


def scatter_rows(name, frames, groups, last=True):
    operands = [x for wanted, parts in groups for x in (wanted, *parts)]
    staging = [VMEM(frames.shape, BF16), pltpu.SemaphoreType.DMA((len(chunks_of(frames.shape[0])),))]
    return pl.pallas_call(
        functools.partial(scatter_body, [len(parts) for _, parts in groups]),
        out_shape=jax.ShapeDtypeStruct(frames.shape, BF16),
        in_specs=[vspec()] * (1 + len(operands)),
        out_specs=ANY if last else vspec(),
        scratch_shapes=staging if last else [],
        compiler_params=pltpu.CompilerParams(vmem_limit_bytes=8 * 1024 * 1024),
        name=name,
    )(frames, *operands)


def block_start(step, side, width):
    tensors = lax.axis_size("tensor")
    chip = (lax.axis_index("tensor") + tensors + step) % tensors
    return (chip * 2 + (lax.axis_index("pair") + side) % 2) * width


def assemble(full_ref, blocks, ways, width):
    if len(ways) == 1:
        full_ref[...] = blocks[0][...]
        return
    for (step, side), block in zip(ways, blocks):
        start = pl.multiple_of(block_start(-step, side, width), 128)
        full_ref[:, pl.ds(start, width)] = block[...]


def dissect(total_ref, outs, ways, width):
    if len(ways) == 1:
        outs[0][...] = total_ref[...]
        return
    for (step, side), out in zip(ways, outs):
        start = pl.multiple_of(block_start(step, side, width), 128)
        out[...] = total_ref[:, pl.ds(start, width)]


def forward_body(ways, width, count_ref, picked_ref, *refs):
    n = len(ways)
    blocks = refs[:n]
    up_own, up_sib, down_own, down_sib, gain_ref, router_ref = refs[n : n + 6]
    outs = refs[n + 6 : 2 * n + 6]
    full_ref, stats_ref, hidden_ref, slope_ref = refs[2 * n + 6 : 2 * n + 10]
    mine_ref, sib_ref, total_ref = refs[2 * n + 10 :]
    mine_ref[...], sib_ref[...] = [x.reshape(mine_ref.shape) for x in wanted_slots(count_ref, picked_ref)]
    assemble(full_ref, blocks, ways, width)
    half, features = full_ref.shape
    hidden_dev = up_own.shape[1]
    wide = full_ref[...].astype(F32)
    gate = jax.nn.sigmoid(jnp.sum(wide * router_ref[...].reshape(1, features), axis=1, keepdims=True))
    mean = jnp.sum(wide, axis=1, keepdims=True) * (1.0 / features)
    deviate = wide - mean
    inv = lax.rsqrt(jnp.sum(deviate * deviate, axis=1, keepdims=True) * (1.0 / features) + EPS)
    normed = (deviate * inv * gain_ref[...].reshape(1, features)).astype(BF16)
    lane = lax.broadcasted_iota(jnp.int32, (half, 128), 1)
    stats_ref[...] = jnp.where(lane == 0, mean, jnp.where(lane == 1, inv, gate))
    half_gate = 0.5 * gate
    for i, up in enumerate((up_own, up_sib)):
        value = jnp.dot(normed, up[...], preferred_element_type=F32)
        s = jax.nn.sigmoid(value)
        cols = slice(i * hidden_dev, (i + 1) * hidden_dev)
        hidden_ref[:, cols] = (value * s).astype(BF16)
        slope_ref[:, cols] = half_gate * s * (1.0 + value * (1.0 - s))
    total = jnp.dot(hidden_ref[:, :hidden_dev], down_own[...], preferred_element_type=F32)
    total = total + jnp.dot(hidden_ref[:, hidden_dev:], down_sib[...], preferred_element_type=F32)
    total_ref[...] = (total * half_gate).astype(BF16)
    dissect(total_ref, outs, ways, width)


def forward(count, picked, blocks, ways, weights, gain, router):
    half, width = blocks[0].shape
    features, hidden_dev = weights[0].shape
    piece = jax.ShapeDtypeStruct((half, width), BF16)
    got = call(
        functools.partial(forward_body, ways, width),
        "forward",
        (piece,) * len(ways)
        + (
            jax.ShapeDtypeStruct((half, features), BF16),
            jax.ShapeDtypeStruct((half, 128), F32),
            jax.ShapeDtypeStruct((half, 2 * hidden_dev), BF16),
            jax.ShapeDtypeStruct((half, 2 * hidden_dev), F32),
        )
        + (jax.ShapeDtypeStruct((half,), jnp.int32),) * 2,
        (count, picked, *blocks, *weights, gain, router),
        [vspec()] * (len(blocks) + 8),
        [VMEM((half, features), BF16)],
        1,
        1,
        16,
    )
    return got[: len(ways)], got[len(ways) : -2], got[-2:]


def backward_body(ways, width, *refs):
    n = len(ways)
    blocks = refs[:n]
    up_own, up_sib, down_own, down_sib, gain_ref, router_ref = refs[n : n + 6]
    full_ref, stats_ref, hidden_ref, slope_ref = refs[n + 6 : n + 10]
    outs = refs[n + 10 : 2 * n + 10]
    (cot_ref,) = refs[2 * n + 10 :]
    assemble(cot_ref, blocks, ways, width)
    half, features = full_ref.shape
    hidden_dev = up_own.shape[1]
    score, pre = 0.0, []
    for i, down in enumerate((down_own, down_sib)):
        value = lax.dot_general(cot_ref[...], down[...], OVER_LANES, preferred_element_type=F32)
        cols = slice(i * hidden_dev, (i + 1) * hidden_dev)
        pre.append((value * slope_ref[:, cols]).astype(BF16))
        score = score + jnp.sum(value * hidden_ref[:, cols].astype(F32), axis=1, keepdims=True)
    scaled = lax.dot_general(pre[0], up_own[...], OVER_LANES, preferred_element_type=F32)
    scaled = scaled + lax.dot_general(pre[1], up_sib[...], OVER_LANES, preferred_element_type=F32)
    scaled = scaled * gain_ref[...].reshape(1, features)
    mean, inv, gate = stats_ref[:, 0:1], stats_ref[:, 1:2], stats_ref[:, 2:3]
    centred = (full_ref[...].astype(F32) - mean) * inv
    plain = jnp.sum(scaled, axis=1, keepdims=True) * (1.0 / features)
    cross = jnp.sum(scaled * centred, axis=1, keepdims=True) * (1.0 / features)
    term = 0.5 * score * gate * (1.0 - gate)
    cot_ref[...] = (inv * (scaled - plain - centred * cross) + term * router_ref[...].reshape(1, features)).astype(BF16)
    dissect(cot_ref, outs, ways, width)


def backward(blocks, ways, weights, gain, router, saved):
    half, width = blocks[0].shape
    features, hidden_dev = weights[0].shape
    return call(
        functools.partial(backward_body, ways, width),
        "backward",
        (jax.ShapeDtypeStruct((half, width), BF16),) * len(ways),
        (*blocks, *weights, gain, router, *saved),
        [vspec()] * (len(blocks) + 10),
        [VMEM((half, features), BF16)],
        1,
        1,
        16,
    )


def after(value, *others):
    return lax.optimization_barrier((value, *others))[0]


def per_device(frames, router_weight, norm_gain, up_weight, down_weight, picked_rows, picked_count, cotangent):
    width = frames.shape[1]
    features = up_weight.shape[0]
    half = picked_rows.shape[0] // 2
    tensors = lax.axis_size("tensor")
    gain, router = norm_gain, router_weight
    steps = range(1, tensors)
    aligned = width % 128 == 0
    pieces = [(0, 0), (0, 1)] + [(k, 0) for k in steps] + [(k, 1) for k in steps]
    ways = pieces if aligned else [(0, 0)]

    def send(x, k, side):
        pairs = [
            (chip * 2 + core, (chip + k) % tensors * 2 + (core + side) % 2) for chip in range(tensors) for core in (0, 1)
        ]
        return lax.ppermute(x, ("tensor", "pair"), pairs)

    def swap(x):
        return lax.ppermute(x, "pair", [(0, 1), (1, 0)])

    def joined(blocks):
        if aligned:
            return blocks
        full = jnp.zeros((half, features), BF16)
        for (k, side), block in zip(pieces, blocks):
            full = lax.dynamic_update_slice_in_dim(full, block, block_start(-k, side, width), 1)
        return [full]

    def cut(outs):
        if aligned:
            return outs
        return [lax.dynamic_slice_in_dim(outs[0], block_start(k, side, width), width, 1) for k, side in pieces]

    def collect(mine, sib, near):
        return [mine, swap(near)] + [send(mine, k, 0) for k in steps] + [send(sib, k, 1) for k in steps]

    def deliver(parts):
        count = tensors - 1
        far_mine = [send(x, k, 0) for x, k in zip(parts[2 : 2 + count], steps)]
        far_sib = [send(x, k, 1) for x, k in zip(parts[2 + count :], steps)]
        return [parts[0]] + far_mine, [swap(parts[1])] + far_sib

    first = lax.axis_index("pair") == 0
    places_mine = jnp.where(first, picked_rows[:half], picked_rows[half:])
    places_sib = jnp.where(first, picked_rows[half:], picked_rows[:half])
    found = (lax.broadcasted_iota(jnp.int32, (frames.shape[0], 1), 0) == picked_rows).astype(BF16)
    rows = lax.dot_general(found, frames, (((0,), (0,)), ((), ())), preferred_element_type=F32).astype(BF16)
    mine = jnp.where(first, rows[:half], rows[half:])
    sib = jnp.where(first, rows[half:], rows[:half])
    up_sib, down_sib = swap(up_weight), swap(after(down_weight, mine))
    blocks = collect(mine, sib, after(sib, up_sib))
    weights = (up_weight, up_sib, down_weight, down_sib)
    rows = lax.dot_general(found, cotangent, (((0,), (0,)), ((), ())), preferred_element_type=F32).astype(BF16)
    cot_mine = jnp.where(first, rows[:half], rows[half:])
    cot_sib = jnp.where(first, rows[half:], rows[:half])
    cot_mine, cot_sib = after(cot_mine, up_sib), after(cot_sib, up_sib, down_sib)
    cot_blocks = collect(cot_mine, cot_sib, cot_sib)
    parts, saved, wanted = forward(picked_count, picked_rows, joined(blocks), ways, weights, gain, router)
    out_mine, out_sib = deliver(cut(parts))
    grads = backward(joined(cot_blocks), ways, weights, gain, router, saved)
    grad_mine, grad_sib = deliver(cut(grads))
    mixed = scatter_rows("mixed_rows", frames, [(wanted[0], out_mine), (wanted[1], out_sib)])
    grad_mine[0] = after(grad_mine[0], mixed)
    started = scatter_rows("grad_rows_mine", cotangent, [(wanted[0], grad_mine)], last=False)
    frames_grad = scatter_rows("grad_rows", started, [(wanted[1], grad_sib)])
    return (mixed, frames_grad)


def solution(mesh):
    return jax.shard_map(
        per_device,
        mesh=mesh,
        in_specs=(
            P(("group", "tm"), ("tensor", "pair")),
            P(),
            P(),
            P(None, ("tensor", "pair")),
            P(("tensor", "pair"), None),
            P(("group", "tm")),
            P("group"),
            P(("group", "tm"), ("tensor", "pair")),
        ),
        out_specs=(P(("group", "tm"), ("tensor", "pair")), P(("group", "tm"), ("tensor", "pair"))),
        check_vma=False,
    )
```
